32 devices in a mesh: segment: 4 (over y, x), lon: 8 (over z, core).
Axes of the slice: x: 2, y: 2, z: 4, core: 2. Of those that a mesh axis runs over, the one named last changes fastest.
Arguments:
- patches: bfloat16 [4, 1, 64, 640], P(None, None, 'lon'), may hold values from -4 to 4
- encoder_weight: bfloat16 [640, 1024], replicated, may hold values from -4 to 4
- layer_weights: bfloat16 [4, 4, 1024, 1024], P('segment'), may hold values from -0.1875 to 0.1875
- layer_gains: float32 [4, 1024], P('segment'), may hold values from 0.25 to 1.75
- final_gain: float32 [1024], replicated, may hold values from 0.25 to 1.75
- decoder_weight: bfloat16 [1024, 640], replicated, may hold values from -0.1875 to 0.1875
Outputs:
- forecast: float32 [4, 1, 64, 640], P('segment', None, 'lon')
The draws below stay inside these ranges and needn't reach their ends.
All inputs are finite; a program needn't handle non-finite values.
Results may differ from the reference program's by a relative error of at most 0.015.
Values may be sent and summed in bfloat16 or wider, within the bound.
No kernel may reach another device: no remote copies, remote signals or barrier semaphores. Data moves between devices by JAX's collectives and lax.ppermute only.
A program may use at most 64 MiB of HBM per device.

```python
import math
import jax
import jax.numpy as jnp
from jax import lax

WIDTH = 1024
HEADS = 16
HEAD_DIM = 64
PATCH_VALUES = 640
BAND = 1
BANDS = 4
LAYERS = 4
LON = 64


def draw_patches(key, part):
    value_key, scale_key = jax.random.split(key, 2)
    shape_all = (BANDS, BAND, LON, PATCH_VALUES)
    shape_rows = (BANDS, BAND, LON, 1)
    values = jnp.clip(jax.random.normal(value_key, shape_all, jnp.float32), -4.0, 4.0)
    scales = jnp.exp(jax.random.uniform(scale_key, shape_rows, jnp.float32, math.log(0.1), math.log(1.0)))
    return (values * scales).astype(jnp.bfloat16)


def draw_encoder_weight(key, part):
    value_key, scale_key = jax.random.split(key)
    shape_all = (PATCH_VALUES, WIDTH)
    values = jnp.clip(jax.random.normal(value_key, shape_all, jnp.float32), -4.0, 4.0)
    scales = jnp.exp(jax.random.uniform(scale_key, (1, WIDTH), jnp.float32, math.log(0.3), math.log(3.0)))
    return (values * scales * PATCH_VALUES ** (-0.5)).astype(jnp.bfloat16)


def block_levels(own_key, shape, pieces, low, high):
    level, own = 1.0, jax.random.fold_in(own_key, 6)
    for dim, blocks in pieces:
        heights = jnp.exp(jax.random.uniform(jax.random.fold_in(own, dim), (blocks,), jnp.float32, low / len(pieces), high / len(pieces)))
        level = level * jnp.repeat(heights, shape[dim] // blocks).reshape([-1 if axis == dim else 1 for axis in range(len(shape))])
    return level


def centred(rng, shape, spread, most, cuts=(), kind=jnp.bfloat16):
    level = block_levels(rng, shape, cuts, -0.22, 0.18) if cuts else 1.0
    array = jax.random.normal(rng, shape, jnp.float32) * spread * level
    return jnp.minimum(jnp.maximum(array, -most), most).astype(kind)


def setup_inputs(seed: int = 0) -> dict:
    key_list = jax.random.split(jax.random.key(seed), 7)
    return {
        "patches": draw_patches(jax.random.fold_in(key_list[6], 71), 0),
        "encoder_weight": draw_encoder_weight(jax.random.fold_in(key_list[6], 71), 0),
        "layer_weights": centred(key_list[2], (LAYERS, 4, WIDTH, WIDTH), WIDTH ** -0.5, 0.1875, ((0, 4),)),
        "layer_gains": jnp.clip(1.0 + 0.15 * jax.random.normal(key_list[3], (LAYERS, WIDTH), jnp.float32), 0.25, 1.75),
        "final_gain": jnp.clip(1.0 + 0.15 * jax.random.normal(key_list[4], (WIDTH,), jnp.float32), 0.25, 1.75),
        "decoder_weight": centred(key_list[5], (WIDTH, PATCH_VALUES), WIDTH ** -0.5, 0.1875),
    }


SOFTCAP = 5.0
EPSILON = 1e-06

def norm_rows(latent, gain):
    square = lax.optimization_barrier(jnp.mean(latent * latent, axis=-1, keepdims=True))
    return latent * lax.rsqrt(square + EPSILON) * gain

def attention_layer(latent, weights_layer, gain_layer):
    normed = norm_rows(latent.astype(jnp.float32), gain_layer).astype(jnp.bfloat16)
    flat = normed.reshape(-1, WIDTH)
    queries = jnp.dot(flat, weights_layer[0], preferred_element_type=jnp.float32).astype(jnp.bfloat16)
    keys_all = jnp.dot(flat, weights_layer[1], preferred_element_type=jnp.float32).astype(jnp.bfloat16)
    values_all = jnp.dot(flat, weights_layer[2], preferred_element_type=jnp.float32).astype(jnp.bfloat16)
    queries = queries.reshape(BAND, LON, HEADS, HEAD_DIM).astype(jnp.float32)
    keys_all = keys_all.reshape(BAND, LON, HEADS, HEAD_DIM).astype(jnp.float32)
    values_all = values_all.reshape(BAND, LON, HEADS, HEAD_DIM).astype(jnp.float32)
    scores = jnp.einsum('blhe,bmhe->bhlm', queries, keys_all) * HEAD_DIM ** (-0.5)
    capped = SOFTCAP * jnp.tanh(scores / SOFTCAP)
    raised = jnp.exp(capped)
    probability = (raised / lax.optimization_barrier(jnp.sum(raised, axis=-1, keepdims=True))).astype(jnp.bfloat16)
    attended = jnp.einsum('bhlm,bmhe->blhe', probability.astype(jnp.float32), values_all)
    attended = attended.astype(jnp.bfloat16).reshape(-1, WIDTH)
    mixed = latent.astype(jnp.float32).reshape(-1, WIDTH) + jnp.dot(attended, weights_layer[3], preferred_element_type=jnp.float32)
    return mixed.astype(jnp.bfloat16).reshape(BAND, LON, WIDTH)

def reference(patches, encoder_weight, layer_weights, layer_gains, final_gain, decoder_weight):
    results = []
    for band_index in range(BANDS):
        flat = patches[band_index].reshape(-1, PATCH_VALUES)
        latent = jnp.dot(flat, encoder_weight, preferred_element_type=jnp.float32).astype(jnp.bfloat16)
        latent = latent.reshape(BAND, LON, WIDTH)
        for layer_index in range(LAYERS):
            latent = attention_layer(latent, layer_weights[layer_index], layer_gains[layer_index])
        final = norm_rows(latent.astype(jnp.float32), final_gain).astype(jnp.bfloat16).reshape(-1, WIDTH)
        decoded = jnp.dot(final, decoder_weight, preferred_element_type=jnp.float32)
        results.append(decoded.reshape(BAND, LON, PATCH_VALUES))
    return jnp.stack(results)
```

```python
import functools

import jax
import jax.numpy as jnp
from jax import lax
from jax.experimental import pallas as pl
from jax.experimental.pallas import tpu as pltpu
from jax.sharding import PartitionSpec as P

HEADS = 16
SOFTCAP = 5.0
EPSILON = 1e-06
BOTH = ("segment", "lon")
VMEM_SPEC = pl.BlockSpec(memory_space=pltpu.VMEM)
SMEM_SPEC = pl.BlockSpec(memory_space=pltpu.SMEM)


def matmul(left, right):
    return jnp.dot(left, right, preferred_element_type=jnp.float32)


def norm_rows(latent, gain):
    square = jnp.mean(latent * latent, axis=-1, keepdims=True)
    return (latent * lax.rsqrt(square + EPSILON) * gain).astype(jnp.bfloat16)


def attend(queries, keys, values):
    rows, width = queries.shape
    head_size = width // HEADS
    heads = min(4, HEADS)
    lanes = heads * head_size
    lane_head = lax.broadcasted_iota(jnp.int32, (rows, lanes), 1) // head_size
    own = [lane_head == head for head in range(heads)]
    row_head = lax.broadcasted_iota(jnp.int32, (heads * rows, heads * rows), 0) // rows
    column_head = lax.broadcasted_iota(jnp.int32, (heads * rows, heads * rows), 1) // rows
    same_head = jnp.where(row_head == column_head, 1.0, 0.0).astype(jnp.bfloat16)
    outs = []
    for start in range(0, width, lanes):
        cut = slice(start, start + lanes)
        zero = jnp.zeros((rows, lanes), jnp.bfloat16)
        key_block = jnp.concatenate([jnp.where(mask, keys[:, cut], zero) for mask in own], axis=0)
        value_block = jnp.concatenate([jnp.where(mask, values[:, cut], zero) for mask in own], axis=0)
        scores = lax.dot_general(
            queries[:, cut], key_block, (((1,), (1,)), ((), ())), preferred_element_type=jnp.float32
        )
        raised = jnp.exp(SOFTCAP * jnp.tanh(scores * (head_size ** (-0.5) / SOFTCAP)))
        high = raised.astype(jnp.bfloat16)
        low = (raised - high.astype(jnp.float32)).astype(jnp.bfloat16)
        total = matmul(high, same_head) + matmul(low, same_head)
        probability = (raised / total).astype(jnp.bfloat16)
        outs.append(matmul(probability, value_block).astype(jnp.bfloat16))
    return jnp.concatenate(outs, axis=-1)


def layer(latent, weights, gain):
    wide = latent.astype(jnp.float32)
    normed = norm_rows(wide, gain)
    queries, keys, values = [matmul(normed, weights[i]).astype(jnp.bfloat16) for i in range(3)]
    attended = attend(queries, keys, values)
    return (wide + matmul(attended, weights[3])).astype(jnp.bfloat16)


def first_kernel(place, patches, encoder, weights, gain, out):
    @pl.when(place[0] == 1)
    def _():
        latent = matmul(patches[...], encoder[...]).astype(jnp.bfloat16)
        out[...] = layer(latent, weights, gain[...])


def middle_kernel(place, latent, weights, gain, out):
    @pl.when(place[0] == 1)
    def _():
        out[...] = layer(latent[...], weights, gain[...])


def last_kernel(group, place, latent, weights, gain, final_gain, decoder, *rest):
    outs, decoded = rest[:-1], rest[-1]

    @pl.when(place[0] == 1)
    def _():
        mixed = layer(latent[...], weights, gain[...])
        final = norm_rows(mixed.astype(jnp.float32), final_gain[...])
        decoded[...] = matmul(final, decoder[...])
        rows = outs[0].shape[0]
        for index, out in enumerate(outs):
            start = pl.multiple_of((index * group + place[1]) * rows, 8)
            out[...] = decoded[pl.ds(start, rows), :]


def in_vmem(value):
    return pltpu.with_memory_space_constraint(value, pltpu.VMEM)


def call(kernel, out_shape, place, operands, scratch=()):
    return pl.pallas_call(
        kernel,
        out_shape=out_shape,
        in_specs=[SMEM_SPEC] + [VMEM_SPEC] * len(operands),
        out_specs=jax.tree.map(lambda _: VMEM_SPEC, out_shape),
        scratch_shapes=list(scratch),
        compiler_params=pltpu.CompilerParams(vmem_limit_bytes=24 * 1024 * 1024),
    )(place, *operands)


def body(patches, encoder_weight, layer_weights, layer_gains, final_gain, decoder_weight):
    segments = lax.axis_size("segment")
    lons = lax.axis_size("lon")
    segment_id = lax.axis_index("segment")
    lon_id = lax.axis_index("lon")
    bands, band_rows, lon_local, patch_values = patches.shape
    assert band_rows == 1 and bands == segments and lons % bands == 0
    group = lons // bands
    columns = lons * lon_local
    width = encoder_weight.shape[1]
    out_values = decoder_weight.shape[1]

    weights = in_vmem(layer_weights[0])
    gain = layer_gains
    member = lon_id % group

    sent = jnp.repeat(patches[:, 0], group, axis=0)
    circle = lax.all_to_all(sent, "lon", 0, 0, tiled=True).reshape(columns, patch_values)

    latent_shape = jax.ShapeDtypeStruct((columns, width), jnp.bfloat16)
    latent = None
    for tick in range(segments):
        place = jnp.stack([(segment_id == tick).astype(jnp.int32), member.astype(jnp.int32)])
        if tick == 0:
            latent = call(
                first_kernel, latent_shape, place, [circle, in_vmem(encoder_weight), weights, gain]
            )
        elif tick < segments - 1:
            latent = call(middle_kernel, latent_shape, place, [latent, weights, gain])
        if tick < segments - 1:
            pairs = [(tick * lons + i, (tick + 1) * lons + i) for i in range(lons)]
            latent = lax.ppermute(latent, BOTH, pairs)
            continue
        part_shape = jax.ShapeDtypeStruct((lon_local, out_values), jnp.float32)
        parts = call(
            functools.partial(last_kernel, group),
            [part_shape] * bands,
            place,
            [latent, weights, gain, final_gain[None], in_vmem(decoder_weight)],
            [pltpu.VMEM((columns, out_values), jnp.float32)],
        )
    received = []
    for index, part in enumerate(parts):
        pairs = [
            ((segments - 1) * lons + band * group + i, band * lons + index * group + i)
            for band in range(bands)
            for i in range(group)
        ]
        received.append(lax.ppermute(part, BOTH, pairs))
    return sum(received[1:], received[0])[None, None]


def solution(mesh):
    in_specs = (
        P(None, None, "lon", None),
        P(),
        P("segment", None, None, None),
        P("segment", None),
        P(),
        P(),
    )
    out_specs = P("segment", None, "lon", None)
    return jax.shard_map(body, mesh=mesh, in_specs=in_specs, out_specs=out_specs, check_vma=False)
```

```python
import functools

import jax
import jax.numpy as jnp
from jax import lax
from jax.experimental import pallas as pl
from jax.experimental.pallas import tpu as pltpu
from jax.sharding import PartitionSpec as P

HEADS = 16
SOFTCAP = 5.0
EPSILON = 1e-06
BOTH = ("segment", "lon")
VMEM_SPEC = pl.BlockSpec(memory_space=pltpu.VMEM)


def matmul(left, right):
    return jnp.dot(left, right, preferred_element_type=jnp.float32)


def norm_rows(latent, gain):
    square = jnp.mean(latent * latent, axis=-1, keepdims=True)
    return (latent * lax.rsqrt(square + EPSILON) * gain).astype(jnp.bfloat16)


def attend(queries, keys, values):
    rows, width = queries.shape
    head_size = width // HEADS
    heads = min(4, HEADS)
    lanes = heads * head_size
    lane_head = lax.broadcasted_iota(jnp.int32, (rows, lanes), 1) // head_size
    own = [lane_head == head for head in range(heads)]
    row_head = lax.broadcasted_iota(jnp.int32, (heads * rows, heads * rows), 0) // rows
    column_head = lax.broadcasted_iota(jnp.int32, (heads * rows, heads * rows), 1) // rows
    same_head = jnp.where(row_head == column_head, 1.0, 0.0).astype(jnp.bfloat16)
    outs = []
    for start in range(0, width, lanes):
        cut = slice(start, start + lanes)
        zero = jnp.zeros((rows, lanes), jnp.bfloat16)
        key_block = jnp.concatenate([jnp.where(mask, keys[:, cut], zero) for mask in own], axis=0)
        value_block = jnp.concatenate([jnp.where(mask, values[:, cut], zero) for mask in own], axis=0)
        scores = lax.dot_general(
            queries[:, cut], key_block, (((1,), (1,)), ((), ())), preferred_element_type=jnp.float32
        )
        raised = jnp.exp(SOFTCAP * jnp.tanh(scores * (head_size ** (-0.5) / SOFTCAP)))
        high = raised.astype(jnp.bfloat16)
        low = (raised - high.astype(jnp.float32)).astype(jnp.bfloat16)
        total = matmul(high, same_head) + matmul(low, same_head)
        probability = (raised / total).astype(jnp.bfloat16)
        outs.append(matmul(probability, value_block).astype(jnp.bfloat16))
    return jnp.concatenate(outs, axis=-1)


def layer(latent, weights, gain):
    wide = latent.astype(jnp.float32)
    normed = norm_rows(wide, gain)
    queries, keys, values = [matmul(normed, weights[i]).astype(jnp.bfloat16) for i in range(3)]
    attended = attend(queries, keys, values)
    return (wide + matmul(attended, weights[3])).astype(jnp.bfloat16)


def load_kernel(*refs):
    count = (len(refs) - 1) // 2
    sources, targets, sems = refs[:count], refs[count:-1], refs[-1]
    copies = []
    for source, target in zip(sources, targets):
        for part in range(source.shape[0]):
            sem = sems.at[len(copies)]
            copies.append(pltpu.make_async_copy(source.at[part], target.at[part], sem))
    for copy in copies:
        copy.start()
    for copy in copies:
        copy.wait()


def load(arrays):
    size = sum(value.size * value.dtype.itemsize for value in arrays)
    return pl.pallas_call(
        load_kernel,
        out_shape=[pltpu.VMEM(value.shape, value.dtype) for value in arrays],
        in_specs=[pl.BlockSpec(memory_space=pltpu.HBM)] * len(arrays),
        out_specs=[VMEM_SPEC] * len(arrays),
        scratch_shapes=[pltpu.SemaphoreType.DMA((sum(value.shape[0] for value in arrays),))],
        compiler_params=pltpu.CompilerParams(vmem_limit_bytes=1024 * 1024),
        cost_estimate=pl.CostEstimate(flops=0, bytes_accessed=2 * size, transcendentals=0),
    )(*[pltpu.with_memory_space_constraint(value, pltpu.HBM) for value in arrays])


def first_kernel(*refs):
    pieces, (encoder, weights, gain, out) = refs[:-4], refs[-4:]

    @pl.when(lax.axis_index("segment") == 0)
    def _():
        patches = jnp.concatenate([piece[...] for piece in pieces], axis=0)
        latent = matmul(patches, encoder[0]).astype(jnp.bfloat16)
        out[...] = layer(latent, weights, gain[...])


def middle_kernel(tick, latent, weights, gain, out):
    @pl.when(lax.axis_index("segment") == tick)
    def _():
        out[...] = layer(latent[...], weights, gain[...])


def last_kernel(tick, group, rows, latent, weights, gain, final_gain, decoder, *rest):
    outs, decoded = rest[:-1], rest[-1]

    @pl.when(lax.axis_index("segment") == tick)
    def _():
        mixed = layer(latent[...], weights, gain[...])
        final = norm_rows(mixed.astype(jnp.float32), final_gain[...])
        decoded[...] = matmul(final, decoder[0])
        for index, out in enumerate(outs):
            start = index * group * rows
            out[...] = decoded[start : start + rows, :]


def in_vmem(value):
    return pltpu.with_memory_space_constraint(value, pltpu.VMEM)


def call(kernel, out_shape, operands, scratch=()):
    return pl.pallas_call(
        kernel,
        out_shape=out_shape,
        in_specs=[VMEM_SPEC] * len(operands),
        out_specs=jax.tree.map(lambda _: VMEM_SPEC, out_shape),
        scratch_shapes=list(scratch),
        compiler_params=pltpu.CompilerParams(vmem_limit_bytes=8 * 1024 * 1024),
    )(*operands)


def everywhere(segments, lons, mask):
    return [(s * lons + i, s * lons + (i ^ mask)) for s in range(segments) for i in range(lons)]


def body(patches, encoder_weight, layer_weights, layer_gains, final_gain, decoder_weight):
    segments = lax.axis_size("segment")
    lons = lax.axis_size("lon")
    bands, band_rows, lon_local, patch_values = patches.shape
    assert band_rows == 1 and bands == segments and lons % bands == 0
    assert lons & (lons - 1) == 0 and bands & (bands - 1) == 0
    group = lons // bands
    columns = lons * lon_local
    width = encoder_weight.shape[1]
    out_values = decoder_weight.shape[1]

    band = lax.axis_index("lon") // group
    held = patches[:, 0]
    step = 1
    while step < group:
        other = lax.ppermute(held, BOTH, everywhere(segments, lons, step))
        held = jnp.concatenate([held, other], axis=1)
        step *= 2
    pieces = [lax.dynamic_index_in_dim(held, band, 0, keepdims=False)]
    for k in range(1, bands):
        sent = lax.dynamic_index_in_dim(held, band ^ k, 0, keepdims=False)
        pieces.append(lax.ppermute(sent, BOTH, everywhere(segments, lons, k * group)))

    loaded = load([layer_weights[0], encoder_weight[None], decoder_weight[None], layer_gains, final_gain[None]])
    weights, encoder, decoder, gain, final_gain = [in_vmem(value) for value in loaded]

    latent_shape = jax.ShapeDtypeStruct((columns, width), jnp.bfloat16)
    part_shape = jax.ShapeDtypeStruct((lon_local, out_values), jnp.float32)
    latent = call(first_kernel, latent_shape, pieces + [encoder, weights, gain])
    for tick in range(1, segments):
        pairs = [((tick - 1) * lons + i, tick * lons + i) for i in range(lons)]
        latent = lax.ppermute(latent, BOTH, pairs)
        if tick < segments - 1:
            latent = call(functools.partial(middle_kernel, tick), latent_shape, [latent, weights, gain])
    parts = call(
        functools.partial(last_kernel, segments - 1, group, lon_local),
        [part_shape] * bands,
        [latent, weights, gain, final_gain, decoder],
        [pltpu.VMEM((columns, out_values), jnp.float32)],
    )
    received = []
    for index, part in enumerate(parts):
        pairs = [
            ((segments - 1) * lons + b * group + i, b * lons + (b ^ index) * group + i)
            for b in range(bands)
            for i in range(group)
        ]
        received.append(lax.ppermute(part, BOTH, pairs))
    return sum(received[1:], received[0])[None, None]


def solution(mesh):
    in_specs = (
        P(None, None, "lon", None),
        P(),
        P("segment", None, None, None),
        P("segment", None),
        P(),
        P(),
    )
    out_specs = P("segment", None, "lon", None)
    return jax.shard_map(body, mesh=mesh, in_specs=in_specs, out_specs=out_specs, check_vma=False)
```

```python
import functools

import jax
import jax.numpy as jnp
from jax import lax
from jax.experimental import pallas as pl
from jax.experimental.pallas import tpu as pltpu
from jax.sharding import PartitionSpec as P

HEADS = 16
SOFTCAP = 5.0
EPSILON = 1e-06
BOTH = ("segment", "lon")
HOP_POWER = 1
OUT_POWER = 1
VMEM_SPEC = pl.BlockSpec(memory_space=pltpu.VMEM)


def matmul(left, right):
    return jnp.dot(left, right, preferred_element_type=jnp.float32)


def norm_rows(latent, gain):
    square = jnp.mean(latent * latent, axis=-1, keepdims=True)
    return (latent * lax.rsqrt(square + EPSILON) * gain).astype(jnp.bfloat16)


def attend(queries, keys, values):
    rows, width = queries.shape
    head_size = width // HEADS
    heads = min(4, HEADS)
    lanes = heads * head_size
    lane_head = lax.broadcasted_iota(jnp.int32, (rows, lanes), 1) // head_size
    own = [lane_head == head for head in range(heads)]
    row_head = lax.broadcasted_iota(jnp.int32, (heads * rows, heads * rows), 0) // rows
    column_head = lax.broadcasted_iota(jnp.int32, (heads * rows, heads * rows), 1) // rows
    same_head = jnp.where(row_head == column_head, 1.0, 0.0).astype(jnp.bfloat16)
    outs = []
    for start in range(0, width, lanes):
        cut = slice(start, start + lanes)
        zero = jnp.zeros((rows, lanes), jnp.bfloat16)
        key_block = jnp.concatenate([jnp.where(mask, keys[:, cut], zero) for mask in own], axis=0)
        value_block = jnp.concatenate([jnp.where(mask, values[:, cut], zero) for mask in own], axis=0)
        scores = lax.dot_general(
            queries[:, cut], key_block, (((1,), (1,)), ((), ())), preferred_element_type=jnp.float32
        )
        raised = jnp.exp(SOFTCAP * jnp.tanh(scores * (head_size ** (-0.5) / SOFTCAP)))
        high = raised.astype(jnp.bfloat16)
        low = (raised - high.astype(jnp.float32)).astype(jnp.bfloat16)
        total = matmul(high, same_head) + matmul(low, same_head)
        probability = (raised / total).astype(jnp.bfloat16)
        outs.append(matmul(probability, value_block).astype(jnp.bfloat16))
    return jnp.concatenate(outs, axis=-1)


def layer(latent, weights, gain):
    wide = latent.astype(jnp.float32)
    normed = norm_rows(wide, gain)
    queries, keys, values = [matmul(normed, weights[i]).astype(jnp.bfloat16) for i in range(3)]
    attended = attend(queries, keys, values)
    return (wide + matmul(attended, weights[3])).astype(jnp.bfloat16)


def load_kernel(*refs):
    count = (len(refs) - 1) // 2
    sources, targets, sems = refs[:count], refs[count:-1], refs[-1]
    copies = []
    for source, target in zip(sources, targets):
        for part in range(source.shape[0]):
            sem = sems.at[len(copies)]
            copies.append(pltpu.make_async_copy(source.at[part], target.at[part], sem))
    for copy in copies:
        copy.start()
    for copy in copies:
        copy.wait()


def load(arrays):
    size = sum(value.size * value.dtype.itemsize for value in arrays)
    return pl.pallas_call(
        load_kernel,
        out_shape=[pltpu.VMEM(value.shape, value.dtype) for value in arrays],
        in_specs=[pl.BlockSpec(memory_space=pltpu.HBM)] * len(arrays),
        out_specs=[VMEM_SPEC] * len(arrays),
        scratch_shapes=[pltpu.SemaphoreType.DMA((sum(value.shape[0] for value in arrays),))],
        compiler_params=pltpu.CompilerParams(vmem_limit_bytes=1024 * 1024),
        cost_estimate=pl.CostEstimate(flops=0, bytes_accessed=2 * size, transcendentals=0),
    )(*[pltpu.with_memory_space_constraint(value, pltpu.HBM) for value in arrays])


def first_kernel(*refs):
    pieces, (encoder, weights, gain, out) = refs[:-4], refs[-4:]

    @pl.when(lax.axis_index("segment") == 0)
    def _():
        patches = jnp.concatenate([piece[...] for piece in pieces], axis=0)
        latent = matmul(patches, encoder[0]).astype(jnp.bfloat16)
        out[...] = layer(latent, weights, gain[...])


def middle_kernel(tick, latent, weights, gain, out):
    @pl.when(lax.axis_index("segment") == tick)
    def _():
        out[...] = layer(latent[...], weights, gain[...])


def last_kernel(tick, group, rows, latent, weights, gain, final_gain, decoder, *rest):
    outs, decoded = rest[:-1], rest[-1]

    @pl.when(lax.axis_index("segment") == tick)
    def _():
        mixed = layer(latent[...], weights, gain[...])
        final = norm_rows(mixed.astype(jnp.float32), final_gain[...])
        decoded[...] = matmul(final, decoder[0])
        for index, out in enumerate(outs):
            start = (index * group + (index == 0)) * rows
            out[...] = decoded[start : start + rows, :]


def in_vmem(value):
    return pltpu.with_memory_space_constraint(value, pltpu.VMEM)


def call(kernel, out_shape, operands, scratch=()):
    return pl.pallas_call(
        kernel,
        out_shape=out_shape,
        in_specs=[VMEM_SPEC] * len(operands),
        out_specs=jax.tree.map(lambda _: VMEM_SPEC, out_shape),
        scratch_shapes=list(scratch),
        compiler_params=pltpu.CompilerParams(vmem_limit_bytes=8 * 1024 * 1024),
    )(*operands)


def assign(cost):
    size = len(cost)
    row_price, column_price, owner = [0.0] * (size + 1), [0.0] * (size + 1), [0] * (size + 1)
    for row in range(1, size + 1):
        owner[0], column = row, 0
        slack, back, seen = [float("inf")] * (size + 1), [0] * (size + 1), [False] * (size + 1)
        while owner[column]:
            seen[column], at, low, best = True, owner[column], float("inf"), 0
            for other in range(1, size + 1):
                if not seen[other]:
                    left = cost[at - 1][other - 1] - row_price[at] - column_price[other]
                    if left < slack[other]:
                        slack[other], back[other] = left, column
                    if slack[other] < low:
                        low, best = slack[other], other
            for other in range(size + 1):
                if seen[other]:
                    row_price[owner[other]] += low
                    column_price[other] -= low
                else:
                    slack[other] -= low
            column = best
        while column:
            owner[column] = owner[back[column]]
            column = back[column]
    chosen = [0] * size
    for column in range(1, size + 1):
        chosen[owner[column] - 1] = column - 1
    return chosen


def apart(one, two):
    return bin(one[0] ^ two[0]).count("1") + abs(one[1] - two[1])


def full_pairs(edges, segments, groups, group, cross, power):
    nodes = [(s, g) for s in range(segments) for g in range(groups)]
    targets = set(edges.values())
    senders = [node for node in nodes if node not in edges]
    takers = [node for node in nodes if node not in targets]
    table = [
        [apart(one, two) ** power + 0.01 if one != two else 0.0 for two in takers] for one in senders
    ]
    filled = {one: takers[column] for one, column in zip(senders, assign(table))}
    pairs = []
    for one in nodes:
        two = edges.get(one) or filled[one]
        flip = 1 if one == two or (cross and one in edges) else 0
        for c in range(group):
            pairs.append(((one[0] * groups + one[1]) * group + c, (two[0] * groups + two[1]) * group + (c ^ flip)))
    return pairs


def everywhere(segments, lons, mask):
    return [(s * lons + i, s * lons + (i ^ mask)) for s in range(segments) for i in range(lons)]


def body(patches, encoder_weight, layer_weights, layer_gains, final_gain, decoder_weight):
    segments = lax.axis_size("segment")
    lons = lax.axis_size("lon")
    bands, band_rows, lon_local, patch_values = patches.shape
    assert band_rows == 1 and bands == segments and lons % bands == 0
    assert lons & (lons - 1) == 0 and bands & (bands - 1) == 0 and 1 < bands < lons
    group = lons // bands
    columns = lons * lon_local
    width = encoder_weight.shape[1]
    out_values = decoder_weight.shape[1]

    place = lax.axis_index("lon") // group
    own = patches[:, 0]
    step = 1
    while step < group:
        other = lax.ppermute(own, BOTH, everywhere(segments, lons, step))
        picked = [lax.dynamic_index_in_dim(own, place ^ k ^ 1, 0, keepdims=False) for k in range(bands)]
        picked = lax.optimization_barrier(picked) if step == 1 else picked
        own = jnp.concatenate([own, other], axis=1)
        step *= 2
    pieces = []
    for k in range(bands):
        theirs = lax.dynamic_index_in_dim(other, place ^ k ^ 1, 0, keepdims=False)
        piece = jnp.concatenate([picked[k], theirs], axis=0)
        pieces.append(lax.ppermute(piece, BOTH, everywhere(segments, lons, k * group + 1)) if k else piece)

    loaded = load([layer_weights[0], encoder_weight[None], decoder_weight[None], layer_gains, final_gain[None]])
    weights, encoder, decoder, gain, final_gain = [in_vmem(value) for value in loaded]

    latent_shape = jax.ShapeDtypeStruct((columns, width), jnp.bfloat16)
    part_shape = jax.ShapeDtypeStruct((lon_local, out_values), jnp.float32)
    latent = call(first_kernel, latent_shape, pieces + [encoder, weights, gain])
    for tick in range(1, segments):
        edges = {(tick - 1, g): (tick, g) for g in range(bands)}
        latent = lax.ppermute(latent, BOTH, full_pairs(edges, segments, bands, group, False, HOP_POWER))
        if tick < segments - 1:
            latent = call(functools.partial(middle_kernel, tick), latent_shape, [latent, weights, gain])
    parts = call(
        functools.partial(last_kernel, segments - 1, group, lon_local),
        [part_shape] * bands,
        [latent, weights, gain, final_gain, decoder],
        [pltpu.VMEM((columns, out_values), jnp.float32)],
    )
    segment_id = lax.axis_index("segment")
    answer = None
    for k, part in enumerate(parts):
        edges = {(segments - 1, g): (g ^ 1, g ^ k) for g in range(bands)}
        taken = lax.ppermute(part, BOTH, full_pairs(edges, segments, bands, group, True, OUT_POWER))
        answer = taken if k == 0 else jnp.where(place ^ segment_id ^ 1 == k, taken, answer)
    return answer[None, None]


def solution(mesh):
    in_specs = (
        P(None, None, "lon", None),
        P(),
        P("segment", None, None, None),
        P("segment", None),
        P(),
        P(),
    )
    out_specs = P("segment", None, "lon", None)
    return jax.shard_map(body, mesh=mesh, in_specs=in_specs, out_specs=out_specs, check_vma=False)
```

```python
import functools

import jax
import jax.numpy as jnp
from jax import lax
from jax.experimental import pallas as pl
from jax.experimental.pallas import tpu as pltpu
from jax.sharding import PartitionSpec as P

HEADS = 16
SOFTCAP = 5.0
EPSILON = 1e-06
BOTH = ("segment", "lon")
HOP_POWER = 1
OUT_POWER = 1
LOG2_E = 1.4426950408889634
FULL_ROWS = 128
EARLY = 2
HBM_SPEC = pl.BlockSpec(memory_space=pltpu.HBM)
VMEM_SPEC = pl.BlockSpec(memory_space=pltpu.VMEM)


def matmul(left, right):
    rows = left.shape[0]
    times = max(1, FULL_ROWS // rows)
    if times > 1:
        left = jnp.concatenate([left] * times, axis=0)
    return jnp.dot(left, right, preferred_element_type=jnp.float32)[:rows]


def norm_rows(latent, gain):
    square = jnp.mean(latent * latent, axis=-1, keepdims=True)
    return (latent * lax.rsqrt(square + EPSILON) * gain).astype(jnp.bfloat16)


def attend(queries, keys, values):
    rows, width = queries.shape
    head_size = width // HEADS
    heads = min(4, HEADS)
    lanes = heads * head_size
    cuts = [slice(start, start + lanes) for start in range(0, width, lanes)]
    turned = keys.T
    key_head = lax.broadcasted_iota(jnp.int32, (lanes, rows), 0) // head_size
    value_head = lax.broadcasted_iota(jnp.int32, (rows, lanes), 1) // head_size
    row_head = lax.broadcasted_iota(jnp.int32, (heads * rows, lanes), 0) // rows
    lane_head = lax.broadcasted_iota(jnp.int32, (heads * rows, lanes), 1) // head_size
    same_head = jnp.where(row_head == lane_head, 1.0, 0.0).astype(jnp.bfloat16)
    scores = []
    for cut in cuts:
        part = turned[cut]
        block = [jnp.where(key_head == head, part, jnp.zeros_like(part)) for head in range(heads)]
        scores.append(
            jnp.dot(queries[:, cut], jnp.concatenate(block, axis=1), preferred_element_type=jnp.float32)
        )
    capped = jnp.tanh(jnp.concatenate(scores, axis=0) * (head_size ** (-0.5) / SOFTCAP))
    raised = jnp.exp2(capped * (SOFTCAP * LOG2_E)).astype(jnp.bfloat16)
    total = jnp.dot(raised, same_head, preferred_element_type=jnp.float32)
    outs = []
    for index, cut in enumerate(cuts):
        part = values[:, cut]
        block = [jnp.where(value_head == head, part, jnp.zeros_like(part)) for head in range(heads)]
        mine = slice(index * rows, (index + 1) * rows)
        mixed = jnp.dot(raised[mine], jnp.concatenate(block, axis=0), preferred_element_type=jnp.float32)
        outs.append((mixed / total[mine]).astype(jnp.bfloat16))
    return jnp.concatenate(outs, axis=-1)


def layer(latent, weights, gain):
    wide = latent.astype(jnp.float32)
    normed = norm_rows(wide, gain)
    queries, keys, values = [matmul(normed, weights(i)).astype(jnp.bfloat16) for i in range(3)]
    attended = attend(queries, keys, values)
    return (wide + matmul(attended, weights(3))).astype(jnp.bfloat16)


def load_kernel(segments, hint, weights, encoder, decoder, gain, final_gain, *rest):
    weights_out, encoder_out, decoder_out, gain_out, final_out, sems = rest
    segment = lax.axis_index("segment")

    def move(pairs):
        copies = [
            pltpu.make_async_copy(source, target, sems.at[index])
            for index, (source, target) in enumerate(pairs)
        ]
        for copy in copies:
            copy.start()
        for copy in copies:
            copy.wait()

    early = [(weights.at[i], weights_out.at[i]) for i in range(EARLY)] + [(gain, gain_out)]
    late = [(weights.at[i], weights_out.at[i]) for i in range(EARLY, 4)]

    @pl.when(segment == 0)
    def _():
        move([(encoder, encoder_out)] + early)

    @pl.when(segment > 0)
    def _():
        move(early + late)

    @pl.when(segment == segments - 1)
    def _():
        move([(decoder, decoder_out), (final_gain, final_out)])


def load(segments, hint, arrays):
    return pl.pallas_call(
        functools.partial(load_kernel, segments),
        out_shape=[pltpu.VMEM(value.shape, value.dtype) for value in arrays],
        in_specs=[pl.BlockSpec(memory_space=pl.ANY)] + [HBM_SPEC] * len(arrays),
        out_specs=[VMEM_SPEC] * len(arrays),
        scratch_shapes=[pltpu.SemaphoreType.DMA((6,))],
        compiler_params=pltpu.CompilerParams(vmem_limit_bytes=1024 * 1024),
        cost_estimate=pl.CostEstimate(flops=0, bytes_accessed=16 * 1024 * 1024, transcendentals=0),
    )(hint, *[in_hbm(value) for value in arrays])


def first_kernel(*refs):
    pieces, (encoder, weights, all_weights, gain, out, fetched, sems) = refs[:-7], refs[-7:]

    @pl.when(lax.axis_index("segment") == 0)
    def _():
        copies = [
            pltpu.make_async_copy(all_weights.at[i], fetched.at[i - EARLY], sems.at[i - EARLY])
            for i in range(EARLY, 4)
        ]
        for copy in copies:
            copy.start()

        def get(i):
            if i < EARLY:
                return weights[i]
            copies[i - EARLY].wait()
            return fetched[i - EARLY]

        patches = jnp.concatenate([piece[...] for piece in pieces], axis=0)
        latent = matmul(patches, encoder[...]).astype(jnp.bfloat16)
        out[...] = layer(latent, get, gain[...])


def middle_kernel(tick, latent, weights, gain, out):
    @pl.when(lax.axis_index("segment") == tick)
    def _():
        out[...] = layer(latent[...], lambda i: weights[i], gain[...])


def last_kernel(tick, group, rows, latent, weights, gain, final_gain, decoder, *outs):
    @pl.when(lax.axis_index("segment") == tick)
    def _():
        mixed = layer(latent[...], lambda i: weights[i], gain[...])
        final = norm_rows(mixed.astype(jnp.float32), final_gain[...])
        decoded = matmul(final, decoder[...])
        for index, out in enumerate(outs):
            start = (index * group + (index == 0)) * rows
            out[...] = decoded[start : start + rows, :]


def in_hbm(value):
    return pltpu.with_memory_space_constraint(value, pltpu.HBM)


def in_vmem(value):
    return pltpu.with_memory_space_constraint(value, pltpu.VMEM)


def call(kernel, out_shape, operands, in_specs=None, scratch=()):
    return pl.pallas_call(
        kernel,
        out_shape=out_shape,
        in_specs=in_specs or [VMEM_SPEC] * len(operands),
        out_specs=jax.tree.map(lambda _: VMEM_SPEC, out_shape),
        scratch_shapes=list(scratch),
        compiler_params=pltpu.CompilerParams(vmem_limit_bytes=16 * 1024 * 1024),
    )(*operands)


def assign(cost):
    size = len(cost)
    row_price, column_price, owner = [0.0] * (size + 1), [0.0] * (size + 1), [0] * (size + 1)
    for row in range(1, size + 1):
        owner[0], column = row, 0
        slack, back, seen = [float("inf")] * (size + 1), [0] * (size + 1), [False] * (size + 1)
        while owner[column]:
            seen[column], at, low, best = True, owner[column], float("inf"), 0
            for other in range(1, size + 1):
                if not seen[other]:
                    left = cost[at - 1][other - 1] - row_price[at] - column_price[other]
                    if left < slack[other]:
                        slack[other], back[other] = left, column
                    if slack[other] < low:
                        low, best = slack[other], other
            for other in range(size + 1):
                if seen[other]:
                    row_price[owner[other]] += low
                    column_price[other] -= low
                else:
                    slack[other] -= low
            column = best
        while column:
            owner[column] = owner[back[column]]
            column = back[column]
    chosen = [0] * size
    for column in range(1, size + 1):
        chosen[owner[column] - 1] = column - 1
    return chosen


def apart(one, two):
    return bin(one[0] ^ two[0]).count("1") + abs(one[1] - two[1])


def full_pairs(edges, segments, groups, group, cross, power):
    nodes = [(s, g) for s in range(segments) for g in range(groups)]
    targets = set(edges.values())
    senders = [node for node in nodes if node not in edges]
    takers = [node for node in nodes if node not in targets]
    table = [
        [apart(one, two) ** power + 0.01 if one != two else 0.0 for two in takers] for one in senders
    ]
    filled = {one: takers[column] for one, column in zip(senders, assign(table))}
    pairs = []
    for one in nodes:
        two = edges.get(one) or filled[one]
        flip = 1 if one == two or (cross and one in edges) else 0
        for c in range(group):
            pairs.append(((one[0] * groups + one[1]) * group + c, (two[0] * groups + two[1]) * group + (c ^ flip)))
    return pairs


def everywhere(segments, lons, mask):
    return [(s * lons + i, s * lons + (i ^ mask)) for s in range(segments) for i in range(lons)]


def body(patches, encoder_weight, layer_weights, layer_gains, final_gain, decoder_weight):
    segments = lax.axis_size("segment")
    lons = lax.axis_size("lon")
    bands, band_rows, lon_local, patch_values = patches.shape
    assert band_rows == 1 and bands == segments and lons % bands == 0
    assert lons & (lons - 1) == 0 and bands & (bands - 1) == 0 and 1 < bands < lons
    group = lons // bands
    columns = lons * lon_local
    width = encoder_weight.shape[1]
    out_values = decoder_weight.shape[1]

    place = lax.axis_index("lon") // group
    own = patches[:, 0]
    step = 1
    while step < group:
        other = lax.ppermute(own, BOTH, everywhere(segments, lons, step))
        picked = [lax.dynamic_index_in_dim(own, place ^ k ^ 1, 0, keepdims=False) for k in range(bands)]
        picked = lax.optimization_barrier(picked) if step == 1 else picked
        own = jnp.concatenate([own, other], axis=1)
        step *= 2
    pieces = []
    for k in range(bands):
        theirs = lax.dynamic_index_in_dim(other, place ^ k ^ 1, 0, keepdims=False)
        piece = jnp.concatenate([picked[k], theirs], axis=0)
        pieces.append(lax.ppermute(piece, BOTH, everywhere(segments, lons, k * group + 1)) if k else piece)

    every = layer_weights[0]
    loaded = load(segments, pieces[0], [every, encoder_weight, decoder_weight, layer_gains, final_gain[None]])
    weights, encoder, decoder, gain, final_gain = [in_vmem(value) for value in loaded]

    latent_shape = jax.ShapeDtypeStruct((columns, width), jnp.bfloat16)
    part_shape = jax.ShapeDtypeStruct((lon_local, out_values), jnp.float32)
    latent = call(
        first_kernel,
        latent_shape,
        pieces + [encoder, weights, in_hbm(every), gain],
        [VMEM_SPEC] * (bands + 2) + [HBM_SPEC, VMEM_SPEC],
        [pltpu.VMEM((4 - EARLY, width, width), jnp.bfloat16), pltpu.SemaphoreType.DMA((4 - EARLY,))],
    )
    for tick in range(1, segments):
        edges = {(tick - 1, g): (tick, g) for g in range(bands)}
        latent = lax.ppermute(latent, BOTH, full_pairs(edges, segments, bands, group, False, HOP_POWER))
        if tick < segments - 1:
            latent = call(functools.partial(middle_kernel, tick), latent_shape, [latent, weights, gain])
    parts = call(
        functools.partial(last_kernel, segments - 1, group, lon_local),
        [part_shape] * bands,
        [latent, weights, gain, final_gain, decoder],
    )
    segment_id = lax.axis_index("segment")
    answer = None
    for k, part in enumerate(parts):
        edges = {(segments - 1, g): (g ^ 1, g ^ k) for g in range(bands)}
        taken = lax.ppermute(part, BOTH, full_pairs(edges, segments, bands, group, True, OUT_POWER))
        answer = taken if k == 0 else jnp.where(place ^ segment_id ^ 1 == k, taken, answer)
    return answer[None, None]


def solution(mesh):
    in_specs = (
        P(None, None, "lon", None),
        P(),
        P("segment", None, None, None),
        P("segment", None),
        P(),
        P(),
    )
    out_specs = P("segment", None, "lon", None)
    return jax.shard_map(body, mesh=mesh, in_specs=in_specs, out_specs=out_specs, check_vma=False)
```

```python
import functools

import jax
import jax.numpy as jnp
from jax import lax
from jax.experimental import pallas as pl
from jax.experimental.pallas import tpu as pltpu
from jax.sharding import PartitionSpec as P

HEADS = 16
SOFTCAP = 5.0
EPSILON = 1e-06
BOTH = ("segment", "lon")
LOG2_E = 1.4426950408889634
FULL_ROWS = 128
EXCHANGE_FLOPS = 5 * 10**9
EARLY = 2
HBM_SPEC = pl.BlockSpec(memory_space=pltpu.HBM)
VMEM_SPEC = pl.BlockSpec(memory_space=pltpu.VMEM)


def matmul(left, right):
    rows = left.shape[0]
    times = max(1, FULL_ROWS // rows)
    if times > 1:
        left = jnp.concatenate([left] * times, axis=0)
    return jnp.dot(left, right, preferred_element_type=jnp.float32)[:rows]


def norm_rows(latent, gain):
    square = jnp.mean(latent * latent, axis=-1, keepdims=True)
    return (latent * lax.rsqrt(square + EPSILON) * gain).astype(jnp.bfloat16)


def attend(queries, keys, values):
    rows, width = queries.shape
    head_size = width // HEADS
    heads = min(4, HEADS)
    lanes = heads * head_size
    cuts = [slice(start, start + lanes) for start in range(0, width, lanes)]
    turned = keys.T
    key_head = lax.broadcasted_iota(jnp.int32, (lanes, rows), 0) // head_size
    value_head = lax.broadcasted_iota(jnp.int32, (rows, lanes), 1) // head_size
    row_head = lax.broadcasted_iota(jnp.int32, (heads * rows, lanes), 0) // rows
    lane_head = lax.broadcasted_iota(jnp.int32, (heads * rows, lanes), 1) // head_size
    same_head = jnp.where(row_head == lane_head, 1.0, 0.0).astype(jnp.bfloat16)
    scores = []
    for cut in cuts:
        part = turned[cut]
        block = [jnp.where(key_head == head, part, jnp.zeros_like(part)) for head in range(heads)]
        scores.append(
            jnp.dot(queries[:, cut], jnp.concatenate(block, axis=1), preferred_element_type=jnp.float32)
        )
    capped = jnp.tanh(jnp.concatenate(scores, axis=0) * (head_size ** (-0.5) / SOFTCAP))
    raised = jnp.exp2(capped * (SOFTCAP * LOG2_E)).astype(jnp.bfloat16)
    total = jnp.dot(raised, same_head, preferred_element_type=jnp.float32)
    outs = []
    for index, cut in enumerate(cuts):
        part = values[:, cut]
        block = [jnp.where(value_head == head, part, jnp.zeros_like(part)) for head in range(heads)]
        mine = slice(index * rows, (index + 1) * rows)
        mixed = jnp.dot(raised[mine], jnp.concatenate(block, axis=0), preferred_element_type=jnp.float32)
        outs.append((mixed / total[mine]).astype(jnp.bfloat16))
    return jnp.concatenate(outs, axis=-1)


def layer(latent, weights, gain):
    wide = latent.astype(jnp.float32)
    normed = norm_rows(wide, gain)
    queries, keys, values = [matmul(normed, weights(i)).astype(jnp.bfloat16) for i in range(3)]
    attended = attend(queries, keys, values)
    return (wide + matmul(attended, weights(3))).astype(jnp.bfloat16)


def leads(group, segment):
    return (lax.axis_index("segment") == segment) & (lax.rem(lax.axis_index("lon"), group) == 0)


def load_kernel(segments, group, hint, weights, decoder, gain, final_gain, *rest):
    weights_out, decoder_out, gain_out, final_out, sems = rest
    segment = lax.axis_index("segment")
    leader = (lax.rem(lax.axis_index("lon"), group) == 0) | (segment == segments - 1)

    def move(pairs):
        copies = [
            pltpu.make_async_copy(source, target, sems.at[index])
            for index, (source, target) in enumerate(pairs)
        ]
        for copy in copies:
            copy.start()
        for copy in copies:
            copy.wait()

    @pl.when(leader & (segment > 0))
    def _():
        move([(weights.at[i], weights_out.at[i]) for i in range(4)] + [(gain, gain_out)])

    @pl.when(leader & (segment == segments - 1))
    def _():
        move([(decoder, decoder_out), (final_gain, final_out)])


def load(segments, group, hint, arrays):
    return pl.pallas_call(
        functools.partial(load_kernel, segments, group),
        out_shape=[pltpu.VMEM(value.shape, value.dtype) for value in arrays],
        in_specs=[pl.BlockSpec(memory_space=pl.ANY)] + [HBM_SPEC] * len(arrays),
        out_specs=[VMEM_SPEC] * len(arrays),
        scratch_shapes=[pltpu.SemaphoreType.DMA((6,))],
        compiler_params=pltpu.CompilerParams(vmem_limit_bytes=1024 * 1024),
        cost_estimate=pl.CostEstimate(flops=0, bytes_accessed=16 * 1024 * 1024, transcendentals=0),
    )(hint, *[in_hbm(value) for value in arrays])


def piece_kernel(group, table, *refs):
    picked, other, outs = refs[: len(table)], refs[len(table)], refs[len(table) + 1 :]
    place, member = lax.axis_index("lon") // group, lax.rem(lax.axis_index("lon"), group)
    for row, mine, out in zip(table, picked, outs):
        out[...] = jnp.concatenate([mine[...], other[place ^ sent_way(row, member) ^ 1]], axis=0)


def sent_way(row, member):
    way = row[1]
    for c in range(1, len(row)):
        way = jnp.where(member == c, row[c ^ 1], way)
    return way


def exchange_table(groups, group):
    count = -(-(groups - 1) // group)
    table = [[0] * group for _ in range(count)]
    ways = list(range(1, groups))
    for step in reversed(range(count)):
        for c in range(group if step == 0 else min(group, len(ways) - step * group)):
            if ways:
                table[step][c] = ways.pop(0)
    return table


def first_kernel(group, *refs):
    pieces, (encoder, weights, gain, out) = refs[:-4], refs[-4:]

    @pl.when(leads(group, 0))
    def _():
        patches = jnp.concatenate([piece[...] for piece in pieces], axis=0)
        latent = matmul(patches, encoder[...]).astype(jnp.bfloat16)
        out[...] = layer(latent, lambda i: weights[i], gain[...])


def middle_kernel(tick, group, latent, weights, gain, out):
    @pl.when(leads(group, tick))
    def _():
        out[...] = layer(latent[...], lambda i: weights[i], gain[...])


def last_kernel(tick, group, rows, turns, *refs):
    latents, (weights, gain, final_gain, decoder) = refs[:group], refs[group : group + 4]
    outs, decoded = refs[group + 4 : -1], refs[-1]
    member = lax.rem(lax.axis_index("lon"), group)

    @pl.when(lax.axis_index("segment") == tick)
    def _():
        latent = latents[0][...]
        for c in range(1, group):
            latent = jnp.where(member == c, latents[c][...], latent)
        mixed = layer(latent, lambda i: weights[i], gain[...])
        final = norm_rows(mixed.astype(jnp.float32), final_gain[...])
        decoded[...] = matmul(final, decoder[...])
        for block, out in enumerate(outs):
            start = pl.multiple_of((block * group + (member ^ turns[block])) * rows, 8)
            out[...] = decoded[pl.ds(start, rows), :]


def in_hbm(value):
    return pltpu.with_memory_space_constraint(value, pltpu.HBM)


def in_vmem(value):
    return pltpu.with_memory_space_constraint(value, pltpu.VMEM)


def call(kernel, out_shape, operands, in_specs=None, scratch=()):
    return pl.pallas_call(
        kernel,
        out_shape=out_shape,
        in_specs=in_specs or [VMEM_SPEC] * len(operands),
        out_specs=jax.tree.map(lambda _: VMEM_SPEC, out_shape),
        scratch_shapes=list(scratch),
        compiler_params=pltpu.CompilerParams(vmem_limit_bytes=16 * 1024 * 1024),
    )(*operands)


def assign(cost):
    size = len(cost)
    row_price, column_price, owner = [0.0] * (size + 1), [0.0] * (size + 1), [0] * (size + 1)
    for row in range(1, size + 1):
        owner[0], column = row, 0
        slack, back, seen = [float("inf")] * (size + 1), [0] * (size + 1), [False] * (size + 1)
        while owner[column]:
            seen[column], at, low, best = True, owner[column], float("inf"), 0
            for other in range(1, size + 1):
                if not seen[other]:
                    left = cost[at - 1][other - 1] - row_price[at] - column_price[other]
                    if left < slack[other]:
                        slack[other], back[other] = left, column
                    if slack[other] < low:
                        low, best = slack[other], other
            for other in range(size + 1):
                if seen[other]:
                    row_price[owner[other]] += low
                    column_price[other] -= low
                else:
                    slack[other] -= low
            column = best
        while column:
            owner[column] = owner[back[column]]
            column = back[column]
    chosen = [0] * size
    for column in range(1, size + 1):
        chosen[owner[column] - 1] = column - 1
    return chosen


def apart(one, two):
    return bin(one[0] ^ two[0]).count("1") + abs(one[1] - two[1])


def full_pairs(edges, segments, groups, group, extra={}):
    devices = [(s, g, c) for s in range(segments) for g in range(groups) for c in range(group)]
    edges = extra | edges
    targets = set(edges.values())
    givers = [one for one in devices if one in targets and one not in edges]
    takers = [one for one in devices if one in edges and one not in targets]
    chosen = assign([[apart(one, two) + 0.0 for two in takers] for one in givers])
    links = edges | {one: takers[column] for one, column in zip(givers, chosen)}
    idle = [one for one in devices if one not in links]
    for s, g, c in idle:
        if (s, g, c ^ 1) in idle:
            links[(s, g, c)] = (s, g, c ^ 1)
    rest = [one for one in idle if one not in links]
    while rest:
        ring = rest[:2] if len(rest) != 3 else rest
        rest = rest[len(ring) :]
        for one, two in zip(ring, ring[1:] + ring[:1]):
            links[one] = two
    number = {one: index for index, one in enumerate(devices)}
    return [(number[one], number[two]) for one, two in links.items()]


def detour(tick, groups):
    links = {}
    for g in range(groups):
        links |= {(tick, g, 0): (tick, g, 1), (tick, g, 1): (tick - 1, g, 1), (tick - 1, g, 1): (tick - 1, g, 0)}
    return links


def everywhere(segments, lons, mask):
    return [(s * lons + i, s * lons + (i ^ mask)) for s in range(segments) for i in range(lons)]


def body(patches, encoder_weight, layer_weights, layer_gains, final_gain, decoder_weight):
    segments = lax.axis_size("segment")
    lons = lax.axis_size("lon")
    bands, band_rows, lon_local, patch_values = patches.shape
    assert band_rows == 1 and bands == segments and lons % bands == 0
    assert lons & (lons - 1) == 0 and bands & (bands - 1) == 0 and 2 < bands < lons
    group = lons // bands
    columns = lons * lon_local
    width = encoder_weight.shape[1]
    out_values = decoder_weight.shape[1]

    place, member = lax.axis_index("lon") // group, lax.axis_index("lon") % group
    table = exchange_table(bands, group)
    rows_sent = [[0] * group] + table
    own = patches[:, 0]
    step = 1
    while step < group:
        other = lax.ppermute(own, BOTH, everywhere(segments, lons, step))
        picked = [
            lax.dynamic_index_in_dim(own, place ^ sent_way(row, member) ^ 1, 0, keepdims=False) for row in rows_sent
        ]
        picked = lax.optimization_barrier(picked) if step == 1 else picked
        own = jnp.concatenate([own, other], axis=1)
        step *= 2
    sent = pl.pallas_call(
        functools.partial(piece_kernel, group, rows_sent),
        out_shape=[jax.ShapeDtypeStruct((group * lon_local, patch_values), jnp.bfloat16)] * len(rows_sent),
        in_specs=[VMEM_SPEC] * (len(rows_sent) + 1),
        out_specs=[VMEM_SPEC] * len(rows_sent),
        compiler_params=pltpu.CompilerParams(vmem_limit_bytes=2 * 1024 * 1024),
        cost_estimate=pl.CostEstimate(flops=EXCHANGE_FLOPS, bytes_accessed=10**6, transcendentals=0),
    )(*picked, other)
    pieces = [sent[0]] + [None] * (bands - 1)
    turns = [1] + [0] * (bands - 1)
    for row, piece in zip(table, sent[1:]):
        pairs = [
            ((s * bands + g) * group + c, (s * bands + (g ^ row[c ^ 1])) * group + (c ^ 1))
            for s in range(segments)
            for g in range(bands)
            for c in range(group)
        ]
        taken = lax.ppermute(piece, BOTH, pairs)
        for c in range(group):
            if row[c]:
                pieces[row[c]] = lax.ppermute(taken, BOTH, everywhere(segments, lons, c)) if c else taken
                turns[row[c]] = c
    loaded = load(segments, group, pieces[0], [layer_weights[0], decoder_weight, layer_gains, final_gain[None]])
    weights, decoder, gain, final_gain = [in_vmem(value) for value in loaded]

    latent_shape = jax.ShapeDtypeStruct((columns, width), jnp.bfloat16)
    part_shape = jax.ShapeDtypeStruct((lon_local, out_values), jnp.float32)
    first = [in_vmem(value) for value in (encoder_weight, layer_weights[0], layer_gains)]
    latent = call(functools.partial(first_kernel, group), latent_shape, pieces + first)
    for tick in range(1, segments - 1):
        edges = {(tick - 1, g, 0): (tick, g, 0) for g in range(bands)}
        latent = lax.ppermute(latent, BOTH, full_pairs(edges, segments, bands, group, detour(tick, bands)))
        latent = call(functools.partial(middle_kernel, tick, group), latent_shape, [latent, weights, gain])
    last = segments - 1
    edges = {(last - 1, g, 0): (last, g, 0) for g in range(bands)}
    latents = [lax.ppermute(latent, BOTH, full_pairs(edges, segments, bands, group, detour(last, bands)))]
    latents += [lax.ppermute(latents[0], BOTH, everywhere(segments, lons, c)) for c in range(1, group)]
    parts = call(
        functools.partial(last_kernel, last, group, lon_local, turns),
        [part_shape] * bands,
        latents + [weights, gain, final_gain, decoder],
        scratch=[pltpu.VMEM((columns, out_values), jnp.float32)],
    )
    segment_id = lax.axis_index("segment")
    answer = None
    for k, part in enumerate(parts):
        edges = {(last, g, c): (g ^ 1, g ^ k, c ^ 1) for g in range(bands) for c in range(group)}
        taken = lax.ppermute(part, BOTH, full_pairs(edges, segments, bands, group))
        answer = taken if k == 0 else jnp.where(place ^ segment_id ^ 1 == k, taken, answer)
    return answer[None, None]


def solution(mesh):
    in_specs = (
        P(None, None, "lon", None),
        P(),
        P("segment", None, None, None),
        P("segment", None),
        P(),
        P(),
    )
    out_specs = P("segment", None, "lon", None)
    return jax.shard_map(body, mesh=mesh, in_specs=in_specs, out_specs=out_specs, check_vma=False)
```

```python
import functools

import jax
import jax.numpy as jnp
from jax import lax
from jax.experimental import pallas as pl
from jax.experimental.pallas import tpu as pltpu
from jax.sharding import PartitionSpec as P

HEADS = 16
SOFTCAP = 5.0
EPSILON = 1e-06
BOTH = ("segment", "lon")
LOG2_E = 1.4426950408889634
FULL_ROWS = 128
EXCHANGE_FLOPS = 5 * 10**9
EARLY = 2
HBM_SPEC = pl.BlockSpec(memory_space=pltpu.HBM)
VMEM_SPEC = pl.BlockSpec(memory_space=pltpu.VMEM)


def matmul(left, right):
    rows = left.shape[0]
    times = max(1, FULL_ROWS // rows)
    if times > 1:
        left = jnp.concatenate([left] * times, axis=0)
    return jnp.dot(left, right, preferred_element_type=jnp.float32)[:rows]


def norm_rows(latent, gain):
    square = jnp.mean(latent * latent, axis=-1, keepdims=True)
    return (latent * lax.rsqrt(square + EPSILON) * gain).astype(jnp.bfloat16)


def attend(queries, keys, values):
    rows, width = queries.shape
    head_size = width // HEADS
    heads = min(4, HEADS)
    lanes = heads * head_size
    cuts = [slice(start, start + lanes) for start in range(0, width, lanes)]
    turned = keys.T
    key_head = lax.broadcasted_iota(jnp.int32, (lanes, rows), 0) // head_size
    value_head = lax.broadcasted_iota(jnp.int32, (rows, lanes), 1) // head_size
    row_head = lax.broadcasted_iota(jnp.int32, (heads * rows, lanes), 0) // rows
    lane_head = lax.broadcasted_iota(jnp.int32, (heads * rows, lanes), 1) // head_size
    same_head = jnp.where(row_head == lane_head, 1.0, 0.0).astype(jnp.bfloat16)
    scores = []
    for cut in cuts:
        part = turned[cut]
        block = [jnp.where(key_head == head, part, jnp.zeros_like(part)) for head in range(heads)]
        scores.append(
            jnp.dot(queries[:, cut], jnp.concatenate(block, axis=1), preferred_element_type=jnp.float32)
        )
    capped = jnp.tanh(jnp.concatenate(scores, axis=0) * (head_size ** (-0.5) / SOFTCAP))
    raised = jnp.exp2(capped * (SOFTCAP * LOG2_E)).astype(jnp.bfloat16)
    total = jnp.dot(raised, same_head, preferred_element_type=jnp.float32)
    outs = []
    for index, cut in enumerate(cuts):
        part = values[:, cut]
        block = [jnp.where(value_head == head, part, jnp.zeros_like(part)) for head in range(heads)]
        mine = slice(index * rows, (index + 1) * rows)
        mixed = jnp.dot(raised[mine], jnp.concatenate(block, axis=0), preferred_element_type=jnp.float32)
        outs.append((mixed / total[mine]).astype(jnp.bfloat16))
    return jnp.concatenate(outs, axis=-1)


def layer(latent, weights, gain):
    wide = latent.astype(jnp.float32)
    normed = norm_rows(wide, gain)
    queries, keys, values = [matmul(normed, weights(i)).astype(jnp.bfloat16) for i in range(3)]
    attended = attend(queries, keys, values)
    return (wide + matmul(attended, weights(3))).astype(jnp.bfloat16)


def leads(group, segment):
    return (lax.axis_index("segment") == segment) & (lax.rem(lax.axis_index("lon"), group) == 0)


def load_kernel(segments, group, hint, weights, decoder, gain, final_gain, *rest):
    weights_out, decoder_out, gain_out, final_out, sems = rest
    segment = lax.axis_index("segment")
    leader = lax.rem(lax.axis_index("lon"), group) == 0

    def move(pairs):
        copies = [
            pltpu.make_async_copy(source, target, sems.at[index])
            for index, (source, target) in enumerate(pairs)
        ]
        for copy in copies:
            copy.start()
        for copy in copies:
            copy.wait()

    @pl.when(leader & (segment > 0))
    def _():
        move([(weights.at[i], weights_out.at[i]) for i in range(4)] + [(gain, gain_out)])

    @pl.when(leader & (segment == segments - 1))
    def _():
        move([(decoder, decoder_out), (final_gain, final_out)])


def load(segments, group, hint, arrays):
    return pl.pallas_call(
        functools.partial(load_kernel, segments, group),
        out_shape=[pltpu.VMEM(value.shape, value.dtype) for value in arrays],
        in_specs=[pl.BlockSpec(memory_space=pl.ANY)] + [HBM_SPEC] * len(arrays),
        out_specs=[VMEM_SPEC] * len(arrays),
        scratch_shapes=[pltpu.SemaphoreType.DMA((6,))],
        compiler_params=pltpu.CompilerParams(vmem_limit_bytes=1024 * 1024),
        cost_estimate=pl.CostEstimate(flops=0, bytes_accessed=16 * 1024 * 1024, transcendentals=0),
    )(hint, *[in_hbm(value) for value in arrays])


def piece_kernel(group, table, *refs):
    picked, other, outs = refs[: len(table)], refs[len(table)], refs[len(table) + 1 :]
    place, member = lax.axis_index("lon") // group, lax.rem(lax.axis_index("lon"), group)
    for row, mine, out in zip(table, picked, outs):
        out[...] = jnp.concatenate([mine[...], other[place ^ sent_way(row, member) ^ 1]], axis=0)


def sent_way(row, member):
    way = row[1]
    for c in range(1, len(row)):
        way = jnp.where(member == c, row[c ^ 1], way)
    return way


def exchange_table(groups, group):
    ways = [2, 1, *range(3, groups)]
    ways += [0] * (-len(ways) % group)
    return [ways[start : start + group] for start in range(0, len(ways), group)]


def first_kernel(group, *refs):
    pieces, (encoder, weights, gain, out) = refs[:-4], refs[-4:]

    @pl.when(leads(group, 0))
    def _():
        patches = jnp.concatenate([piece[...] for piece in pieces], axis=0)
        latent = matmul(patches, encoder[...]).astype(jnp.bfloat16)
        out[...] = layer(latent, lambda i: weights[i], gain[...])


def middle_kernel(tick, group, latent, weights, gain, out):
    @pl.when(leads(group, tick))
    def _():
        out[...] = layer(latent[...], lambda i: weights[i], gain[...])


def last_kernel(tick, group, rows, turns, latent, weights, gain, final_gain, decoder, *outs):
    @pl.when(leads(group, tick))
    def _():
        mixed = layer(latent[...], lambda i: weights[i], gain[...])
        final = norm_rows(mixed.astype(jnp.float32), final_gain[...])
        decoded = matmul(final, decoder[...])
        for block, out in enumerate(outs):
            turn = turns[block] ^ 1 if block else 0
            starts = [(block * group + (c ^ turn)) * rows for c in range(group)]
            out[...] = jnp.concatenate([decoded[start : start + rows] for start in starts], axis=0).astype(out.dtype)


def in_hbm(value):
    return pltpu.with_memory_space_constraint(value, pltpu.HBM)


def in_vmem(value):
    return pltpu.with_memory_space_constraint(value, pltpu.VMEM)


def call(kernel, out_shape, operands, in_specs=None, scratch=()):
    return pl.pallas_call(
        kernel,
        out_shape=out_shape,
        in_specs=in_specs or [VMEM_SPEC] * len(operands),
        out_specs=jax.tree.map(lambda _: VMEM_SPEC, out_shape),
        scratch_shapes=list(scratch),
        compiler_params=pltpu.CompilerParams(vmem_limit_bytes=16 * 1024 * 1024),
    )(*operands)


def assign(cost):
    size = len(cost)
    row_price, column_price, owner = [0.0] * (size + 1), [0.0] * (size + 1), [0] * (size + 1)
    for row in range(1, size + 1):
        owner[0], column = row, 0
        slack, back, seen = [float("inf")] * (size + 1), [0] * (size + 1), [False] * (size + 1)
        while owner[column]:
            seen[column], at, low, best = True, owner[column], float("inf"), 0
            for other in range(1, size + 1):
                if not seen[other]:
                    left = cost[at - 1][other - 1] - row_price[at] - column_price[other]
                    if left < slack[other]:
                        slack[other], back[other] = left, column
                    if slack[other] < low:
                        low, best = slack[other], other
            for other in range(size + 1):
                if seen[other]:
                    row_price[owner[other]] += low
                    column_price[other] -= low
                else:
                    slack[other] -= low
            column = best
        while column:
            owner[column] = owner[back[column]]
            column = back[column]
    chosen = [0] * size
    for column in range(1, size + 1):
        chosen[owner[column] - 1] = column - 1
    return chosen


def apart(one, two):
    return bin(one[0] ^ two[0]).count("1") + abs(one[1] - two[1])


def full_pairs(edges, segments, groups, group, extra={}):
    devices = [(s, g, c) for s in range(segments) for g in range(groups) for c in range(group)]
    edges = extra | edges
    targets = set(edges.values())
    givers = [one for one in devices if one in targets and one not in edges]
    takers = [one for one in devices if one in edges and one not in targets]
    chosen = assign([[apart(one, two) + 0.0 for two in takers] for one in givers])
    links = edges | {one: takers[column] for one, column in zip(givers, chosen)}
    idle = [one for one in devices if one not in links]
    for s, g, c in idle:
        if (s, g, c ^ 1) in idle:
            links[(s, g, c)] = (s, g, c ^ 1)
    rest = [one for one in idle if one not in links]
    while rest:
        ring = rest[:2] if len(rest) != 3 else rest
        rest = rest[len(ring) :]
        for one, two in zip(ring, ring[1:] + ring[:1]):
            links[one] = two
    number = {one: index for index, one in enumerate(devices)}
    return [(number[one], number[two]) for one, two in links.items()]


def detour(tick, groups):
    links = {}
    for g in range(groups):
        links |= {(tick, g, 0): (tick, g, 1), (tick, g, 1): (tick - 1, g, 1), (tick - 1, g, 1): (tick - 1, g, 0)}
    return links


def ring_up(devices, links):
    alone = []
    for one in devices:
        mate = (one[0], one[1], one[2] ^ 1)
        if mate in devices:
            links[one] = mate
        else:
            alone.append(one)
    while len(alone) > 1:
        one, two = min(
            ((one, two) for index, one in enumerate(alone) for two in alone[index + 1 :]), key=lambda pair: apart(*pair)
        )
        links[one], links[two] = two, one
        alone = [three for three in alone if three not in (one, two)]
    for one in alone:
        two = min((two for two in devices if two != one and two[2] == 1), key=lambda two: apart(one, two))
        after = links[two]
        links[one], links[two], links[after] = two, after, one


def fan_pairs(k, segments, groups, group, late):
    last = segments - 1
    devices = [(s, g, c) for s in range(segments) for g in range(groups) for c in range(group)]
    links = {(last, g, 0): (g ^ 1, g ^ k, 1) for g in range(groups)}
    taken = list(links.values())
    outside = [one for one in taken if one[0] != last]
    inside = [one for one in taken if one[0] == last]
    for s, g, c in inside:
        links[(s, g, 1)] = (s, g, 0)
    for s, g, c in outside:
        links[(s, g, 1)] = (s, g, 0)
    givers = [(s, g, 0) for s, g, c in outside]
    takers = [(last, g, 0) for g in range(groups) if (last, g, 1) not in inside]
    waiting = [one for one in late if one[0] == last and one not in links]
    if len(waiting) % 2 and len(waiting) < groups - 1:
        one = waiting[0]
        links[one] = (last, one[1], 0)
        takers[takers.index(links[one])] = one
    for one, column in zip(givers, assign([[apart(one, two) + 0.0 for two in takers] for one in givers])):
        links[one] = takers[column]
    idle = [one for one in devices if one not in links]
    ring_up([one for one in idle if one not in late], links)
    ring_up([one for one in idle if one in late], links)
    late |= {(s, g, c) for s, g, _ in taken for c in range(2)} - {(last, g, 0) for g in range(groups)}
    number = {one: index for index, one in enumerate(devices)}
    assert len(set(links.values())) == len(links) == len(devices)
    return [(number[one], number[two]) for one, two in links.items()]


def everywhere(segments, lons, mask):
    return [(s * lons + i, s * lons + (i ^ mask)) for s in range(segments) for i in range(lons)]


def body(patches, encoder_weight, layer_weights, layer_gains, final_gain, decoder_weight):
    segments = lax.axis_size("segment")
    lons = lax.axis_size("lon")
    bands, band_rows, lon_local, patch_values = patches.shape
    assert band_rows == 1 and bands == segments and lons % bands == 0
    assert lons & (lons - 1) == 0 and bands & (bands - 1) == 0 and 2 < bands < lons
    group = lons // bands
    columns = lons * lon_local
    width = encoder_weight.shape[1]
    out_values = decoder_weight.shape[1]

    place, member = lax.axis_index("lon") // group, lax.axis_index("lon") % group
    table = exchange_table(bands, group)
    rows_sent = [[0] * group] + table
    own = patches[:, 0]
    step = 1
    while step < group:
        other = lax.ppermute(own, BOTH, everywhere(segments, lons, step))
        picked = [
            lax.dynamic_index_in_dim(own, place ^ sent_way(row, member) ^ 1, 0, keepdims=False) for row in rows_sent
        ]
        picked = lax.optimization_barrier(picked) if step == 1 else picked
        own = jnp.concatenate([own, other], axis=1)
        step *= 2
    sent = pl.pallas_call(
        functools.partial(piece_kernel, group, rows_sent),
        out_shape=[jax.ShapeDtypeStruct((group * lon_local, patch_values), jnp.bfloat16)] * len(rows_sent),
        in_specs=[VMEM_SPEC] * (len(rows_sent) + 1),
        out_specs=[VMEM_SPEC] * len(rows_sent),
        compiler_params=pltpu.CompilerParams(vmem_limit_bytes=2 * 1024 * 1024),
        cost_estimate=pl.CostEstimate(flops=EXCHANGE_FLOPS, bytes_accessed=10**6, transcendentals=0),
    )(*picked, other)
    pieces = [sent[0]] + [None] * (bands - 1)
    turns = [1] + [0] * (bands - 1)
    for row, piece in zip(table, sent[1:]):
        pairs = [
            ((s * bands + g) * group + c, (s * bands + (g ^ row[c ^ 1])) * group + (c ^ 1))
            for s in range(segments)
            for g in range(bands)
            for c in range(group)
        ]
        taken = lax.ppermute(piece, BOTH, pairs)
        for c in range(group):
            if row[c]:
                pieces[row[c]] = lax.ppermute(taken, BOTH, everywhere(segments, lons, c)) if c else taken
                turns[row[c]] = c
    loaded = load(segments, group, pieces[0], [layer_weights[0], decoder_weight, layer_gains, final_gain[None]])
    weights, decoder, gain, final_gain = [in_vmem(value) for value in loaded]

    latent_shape = jax.ShapeDtypeStruct((columns, width), jnp.bfloat16)
    part_shape = jax.ShapeDtypeStruct((group * lon_local, out_values), jnp.bfloat16)
    first = [in_vmem(value) for value in (encoder_weight, layer_weights[0], layer_gains)]
    latent = call(functools.partial(first_kernel, group), latent_shape, pieces + first)
    for tick in range(1, segments - 1):
        edges = {(tick - 1, g, 0): (tick, g, 0) for g in range(bands)}
        latent = lax.ppermute(latent, BOTH, full_pairs(edges, segments, bands, group, detour(tick, bands)))
        latent = call(functools.partial(middle_kernel, tick, group), latent_shape, [latent, weights, gain])
    last = segments - 1
    edges = {(last - 1, g, 0): (last, g, 0) for g in range(bands)}
    latent = lax.ppermute(latent, BOTH, full_pairs(edges, segments, bands, group, detour(last, bands)))
    parts = call(
        functools.partial(last_kernel, last, group, lon_local, turns),
        [part_shape] * bands,
        [latent, weights, gain, final_gain, decoder],
    )
    segment_id = lax.axis_index("segment")
    late, picked = set(), None
    ways = {k: fan_pairs(k, segments, bands, group, late) for k in range(bands - 1, -1, -1)}
    for k in (bands - 1, *range(bands - 1)):
        taken = lax.ppermute(parts[k], BOTH, ways[k])
        picked = taken if picked is None else jnp.where(place ^ segment_id ^ 1 == k, taken, picked)
    rows = [picked[c * lon_local : (c + 1) * lon_local] for c in range(group)]
    answer = rows[1]
    for e in range(1, group):
        handed = lax.ppermute(rows[1 ^ e], BOTH, everywhere(segments, lons, e))
        answer = jnp.where(member == 1 ^ e, handed, answer)
    return answer.astype(jnp.float32)[None, None]


def solution(mesh):
    in_specs = (
        P(None, None, "lon", None),
        P(),
        P("segment", None, None, None),
        P("segment", None),
        P(),
        P(),
    )
    out_specs = P("segment", None, "lon", None)
    return jax.shard_map(body, mesh=mesh, in_specs=in_specs, out_specs=out_specs, check_vma=False)
```

```python
import functools

import jax
import jax.numpy as jnp
from jax import lax
from jax.experimental import pallas as pl
from jax.experimental.pallas import tpu as pltpu
from jax.sharding import PartitionSpec as P

HEADS = 16
SOFTCAP = 5.0
EPSILON = 1e-06
BOTH = ("segment", "lon")
LOG2_E = 1.4426950408889634
FULL_ROWS = 128
EXCHANGE_FLOPS = 5 * 10**9
EARLY = 2
HBM_SPEC = pl.BlockSpec(memory_space=pltpu.HBM)
VMEM_SPEC = pl.BlockSpec(memory_space=pltpu.VMEM)


def matmul(left, right):
    rows = left.shape[0]
    times = max(1, FULL_ROWS // rows)
    if times > 1:
        left = jnp.concatenate([left] * times, axis=0)
    return jnp.dot(left, right, preferred_element_type=jnp.float32)[:rows]


def norm_rows(latent, gain):
    square = jnp.mean(latent * latent, axis=-1, keepdims=True)
    return (latent * lax.rsqrt(square + EPSILON) * gain).astype(jnp.bfloat16)


def attend(queries, keys, values):
    rows, width = queries.shape
    head_size = width // HEADS
    heads = min(4, HEADS)
    lanes = heads * head_size
    cuts = [slice(start, start + lanes) for start in range(0, width, lanes)]
    turned = keys.T
    key_head = lax.broadcasted_iota(jnp.int32, (lanes, rows), 0) // head_size
    value_head = lax.broadcasted_iota(jnp.int32, (rows, lanes), 1) // head_size
    row_head = lax.broadcasted_iota(jnp.int32, (heads * rows, lanes), 0) // rows
    lane_head = lax.broadcasted_iota(jnp.int32, (heads * rows, lanes), 1) // head_size
    same_head = jnp.where(row_head == lane_head, 1.0, 0.0).astype(jnp.bfloat16)
    scores = []
    for cut in cuts:
        part = turned[cut]
        block = [jnp.where(key_head == head, part, jnp.zeros_like(part)) for head in range(heads)]
        scores.append(
            jnp.dot(queries[:, cut], jnp.concatenate(block, axis=1), preferred_element_type=jnp.float32)
        )
    capped = jnp.tanh(jnp.concatenate(scores, axis=0) * (head_size ** (-0.5) / SOFTCAP))
    raised = jnp.exp2(capped * (SOFTCAP * LOG2_E)).astype(jnp.bfloat16)
    total = jnp.dot(raised, same_head, preferred_element_type=jnp.float32)
    outs = []
    for index, cut in enumerate(cuts):
        part = values[:, cut]
        block = [jnp.where(value_head == head, part, jnp.zeros_like(part)) for head in range(heads)]
        mine = slice(index * rows, (index + 1) * rows)
        mixed = jnp.dot(raised[mine], jnp.concatenate(block, axis=0), preferred_element_type=jnp.float32)
        outs.append((mixed / total[mine]).astype(jnp.bfloat16))
    return jnp.concatenate(outs, axis=-1)


def layer(latent, weights, gain):
    wide = latent.astype(jnp.float32)
    normed = norm_rows(wide, gain)
    queries, keys, values = [matmul(normed, weights(i)).astype(jnp.bfloat16) for i in range(3)]
    attended = attend(queries, keys, values)
    return (wide + matmul(attended, weights(3))).astype(jnp.bfloat16)


def leads(group, segment):
    return (lax.axis_index("segment") == segment) & (lax.rem(lax.axis_index("lon"), group) == segment % 2)


def load_kernel(segments, group, hint, weights, decoder, gain, final_gain, *rest):
    weights_out, decoder_out, gain_out, final_out, sems = rest
    segment = lax.axis_index("segment")
    leader = lax.rem(lax.axis_index("lon"), group) == lax.rem(segment, 2)

    def move(pairs):
        copies = [
            pltpu.make_async_copy(source, target, sems.at[index])
            for index, (source, target) in enumerate(pairs)
        ]
        for copy in copies:
            copy.start()
        for copy in copies:
            copy.wait()

    @pl.when(leader & (segment > 0))
    def _():
        move([(weights.at[i], weights_out.at[i]) for i in range(4)] + [(gain, gain_out)])

    @pl.when(leader & (segment == segments - 1))
    def _():
        move([(decoder, decoder_out), (final_gain, final_out)])


def load(segments, group, hint, arrays):
    return pl.pallas_call(
        functools.partial(load_kernel, segments, group),
        out_shape=[pltpu.VMEM(value.shape, value.dtype) for value in arrays],
        in_specs=[pl.BlockSpec(memory_space=pl.ANY)] + [HBM_SPEC] * len(arrays),
        out_specs=[VMEM_SPEC] * len(arrays),
        scratch_shapes=[pltpu.SemaphoreType.DMA((6,))],
        compiler_params=pltpu.CompilerParams(vmem_limit_bytes=1024 * 1024),
        cost_estimate=pl.CostEstimate(flops=0, bytes_accessed=16 * 1024 * 1024, transcendentals=0),
    )(hint, *[in_hbm(value) for value in arrays])


def piece_kernel(group, table, *refs):
    picked, other, outs = refs[: len(table)], refs[len(table)], refs[len(table) + 1 :]
    place, member = lax.axis_index("lon") // group, lax.rem(lax.axis_index("lon"), group)
    for row, mine, out in zip(table, picked, outs):
        out[...] = jnp.concatenate([mine[...], other[place ^ sent_way(row, member) ^ 1]], axis=0)


def sent_way(row, member):
    way = row[1]
    for c in range(1, len(row)):
        way = jnp.where(member == c, row[c ^ 1], way)
    return way


def exchange_table(groups, group):
    ways = [2, 1, *range(3, groups)]
    ways += [0] * (-len(ways) % group)
    return [ways[start : start + group] for start in range(0, len(ways), group)]


def first_kernel(group, *refs):
    pieces, (encoder, weights, gain, out) = refs[:-4], refs[-4:]

    @pl.when(leads(group, 0))
    def _():
        patches = jnp.concatenate([piece[...] for piece in pieces], axis=0)
        latent = matmul(patches, encoder[...]).astype(jnp.bfloat16)
        out[...] = layer(latent, lambda i: weights[i], gain[...])


def middle_kernel(tick, group, latent, weights, gain, out):
    @pl.when(leads(group, tick))
    def _():
        out[...] = layer(latent[...], lambda i: weights[i], gain[...])


def last_kernel(tick, group, rows, turns, latent, weights, gain, final_gain, decoder, *outs):
    @pl.when(leads(group, tick))
    def _():
        mixed = layer(latent[...], lambda i: weights[i], gain[...])
        final = norm_rows(mixed.astype(jnp.float32), final_gain[...])
        decoded = matmul(final, decoder[...])
        for block, out in enumerate(outs):
            turn = turns[block] ^ 1 if block else 0
            starts = [(block * group + (c ^ turn)) * rows for c in range(group)]
            out[...] = jnp.concatenate([decoded[start : start + rows] for start in starts], axis=0).astype(out.dtype)


def in_hbm(value):
    return pltpu.with_memory_space_constraint(value, pltpu.HBM)


def in_vmem(value):
    return pltpu.with_memory_space_constraint(value, pltpu.VMEM)


def call(kernel, out_shape, operands, in_specs=None, scratch=()):
    return pl.pallas_call(
        kernel,
        out_shape=out_shape,
        in_specs=in_specs or [VMEM_SPEC] * len(operands),
        out_specs=jax.tree.map(lambda _: VMEM_SPEC, out_shape),
        scratch_shapes=list(scratch),
        compiler_params=pltpu.CompilerParams(vmem_limit_bytes=16 * 1024 * 1024),
    )(*operands)


def assign(cost):
    size = len(cost)
    row_price, column_price, owner = [0.0] * (size + 1), [0.0] * (size + 1), [0] * (size + 1)
    for row in range(1, size + 1):
        owner[0], column = row, 0
        slack, back, seen = [float("inf")] * (size + 1), [0] * (size + 1), [False] * (size + 1)
        while owner[column]:
            seen[column], at, low, best = True, owner[column], float("inf"), 0
            for other in range(1, size + 1):
                if not seen[other]:
                    left = cost[at - 1][other - 1] - row_price[at] - column_price[other]
                    if left < slack[other]:
                        slack[other], back[other] = left, column
                    if slack[other] < low:
                        low, best = slack[other], other
            for other in range(size + 1):
                if seen[other]:
                    row_price[owner[other]] += low
                    column_price[other] -= low
                else:
                    slack[other] -= low
            column = best
        while column:
            owner[column] = owner[back[column]]
            column = back[column]
    chosen = [0] * size
    for column in range(1, size + 1):
        chosen[owner[column] - 1] = column - 1
    return chosen


def apart(one, two):
    return bin(one[0] ^ two[0]).count("1") + abs(one[1] - two[1])


def full_pairs(edges, segments, groups, group, extra={}):
    devices = [(s, g, c) for s in range(segments) for g in range(groups) for c in range(group)]
    edges = extra | edges
    targets = set(edges.values())
    givers = [one for one in devices if one in targets and one not in edges]
    takers = [one for one in devices if one in edges and one not in targets]
    chosen = assign([[apart(one, two) + 0.0 for two in takers] for one in givers])
    links = edges | {one: takers[column] for one, column in zip(givers, chosen)}
    idle = [one for one in devices if one not in links]
    for s, g, c in idle:
        if (s, g, c ^ 1) in idle:
            links[(s, g, c)] = (s, g, c ^ 1)
    rest = [one for one in idle if one not in links]
    while rest:
        ring = rest[:2] if len(rest) != 3 else rest
        rest = rest[len(ring) :]
        for one, two in zip(ring, ring[1:] + ring[:1]):
            links[one] = two
    number = {one: index for index, one in enumerate(devices)}
    return [(number[one], number[two]) for one, two in links.items()]


def detour(tick, groups):
    links = {}
    here, there = tick % 2, (tick - 1) % 2
    for g in range(groups):
        links |= {(tick, g, here): (tick, g, here ^ 1), (tick, g, here ^ 1): (tick - 1, g, there ^ 1)}
        links |= {(tick - 1, g, there ^ 1): (tick - 1, g, there)}
    return links


def ring_up(devices, links, free):
    alone = []
    for one in devices:
        mate = (one[0], one[1], one[2] ^ 1)
        if mate in devices:
            links[one] = mate
        else:
            alone.append(one)
    while len(alone) > 1:
        one, two = min(
            ((one, two) for index, one in enumerate(alone) for two in alone[index + 1 :]), key=lambda pair: apart(*pair)
        )
        links[one], links[two] = two, one
        alone = [three for three in alone if three not in (one, two)]
    for one in alone:
        two = min((two for two in devices if two != one and two[2] == free), key=lambda two: apart(one, two))
        after = links[two]
        links[one], links[two], links[after] = two, after, one


def fan_pairs(k, segments, groups, group, late):
    last = segments - 1
    work = last % 2
    free = work ^ 1
    devices = [(s, g, c) for s in range(segments) for g in range(groups) for c in range(group)]
    links = {(last, g, work): (g ^ 1, g ^ k, free) for g in range(groups)}
    taken = list(links.values())
    for s, g, _ in taken:
        links[(s, g, free)] = (s, g, work)
    inside = [g for s, g, _ in taken if s == last]
    givers = [(s, g, work) for s, g, _ in taken if s != last]
    takers = [(last, g, work) for g in range(groups) if g not in inside]
    waiting = [one for one in sorted(late) if one[0] == last and one not in links]
    if len(waiting) % 2 and len(waiting) < groups - 1:
        one = waiting[0]
        links[one] = (last, one[1], work)
        takers[takers.index(links[one])] = one
    for one, column in zip(givers, assign([[apart(one, two) + 0.0 for two in takers] for one in givers])):
        links[one] = takers[column]
    idle = [one for one in devices if one not in links]
    ring_up([one for one in idle if one not in late], links, free)
    ring_up([one for one in idle if one in late], links, free)
    late |= {(s, g, c) for s, g, _ in taken for c in range(2)} - {(last, g, work) for g in range(groups)}
    number = {one: index for index, one in enumerate(devices)}
    assert len(set(links.values())) == len(links) == len(devices)
    return [(number[one], number[two]) for one, two in links.items()]


def everywhere(segments, lons, mask):
    return [(s * lons + i, s * lons + (i ^ mask)) for s in range(segments) for i in range(lons)]


def body(patches, encoder_weight, layer_weights, layer_gains, final_gain, decoder_weight):
    segments = lax.axis_size("segment")
    lons = lax.axis_size("lon")
    bands, band_rows, lon_local, patch_values = patches.shape
    assert band_rows == 1 and bands == segments and lons % bands == 0
    assert lons & (lons - 1) == 0 and bands & (bands - 1) == 0 and 2 < bands < lons
    group = lons // bands
    columns = lons * lon_local
    width = encoder_weight.shape[1]
    out_values = decoder_weight.shape[1]

    place, member = lax.axis_index("lon") // group, lax.axis_index("lon") % group
    table = exchange_table(bands, group)
    rows_sent = [[0] * group] + table
    own = patches[:, 0]
    step = 1
    while step < group:
        other = lax.ppermute(own, BOTH, everywhere(segments, lons, step))
        picked = [
            lax.dynamic_index_in_dim(own, place ^ sent_way(row, member) ^ 1, 0, keepdims=False) for row in rows_sent
        ]
        picked = lax.optimization_barrier(picked) if step == 1 else picked
        own = jnp.concatenate([own, other], axis=1)
        step *= 2
    sent = pl.pallas_call(
        functools.partial(piece_kernel, group, rows_sent),
        out_shape=[jax.ShapeDtypeStruct((group * lon_local, patch_values), jnp.bfloat16)] * len(rows_sent),
        in_specs=[VMEM_SPEC] * (len(rows_sent) + 1),
        out_specs=[VMEM_SPEC] * len(rows_sent),
        compiler_params=pltpu.CompilerParams(vmem_limit_bytes=2 * 1024 * 1024),
        cost_estimate=pl.CostEstimate(flops=EXCHANGE_FLOPS, bytes_accessed=10**6, transcendentals=0),
    )(*picked, other)
    pieces = [sent[0]] + [None] * (bands - 1)
    turns = [1] + [0] * (bands - 1)
    for row, piece in zip(table, sent[1:]):
        pairs = [
            ((s * bands + g) * group + c, (s * bands + (g ^ row[c ^ 1])) * group + (c ^ 1))
            for s in range(segments)
            for g in range(bands)
            for c in range(group)
        ]
        taken = lax.ppermute(piece, BOTH, pairs)
        for c in range(group):
            if row[c]:
                pieces[row[c]] = lax.ppermute(taken, BOTH, everywhere(segments, lons, c)) if c else taken
                turns[row[c]] = c
    loaded = load(segments, group, pieces[0], [layer_weights[0], decoder_weight, layer_gains, final_gain[None]])
    weights, decoder, gain, final_gain = [in_vmem(value) for value in loaded]

    latent_shape = jax.ShapeDtypeStruct((columns, width), jnp.bfloat16)
    part_shape = jax.ShapeDtypeStruct((group * lon_local, out_values), jnp.bfloat16)
    first = [in_vmem(value) for value in (encoder_weight, layer_weights[0], layer_gains)]
    latent = call(functools.partial(first_kernel, group), latent_shape, pieces + first)
    for tick in range(1, segments - 1):
        edges = {(tick - 1, g, (tick - 1) % 2): (tick, g, tick % 2) for g in range(bands)}
        latent = lax.ppermute(latent, BOTH, full_pairs(edges, segments, bands, group, detour(tick, bands)))
        latent = call(functools.partial(middle_kernel, tick, group), latent_shape, [latent, weights, gain])
    last = segments - 1
    edges = {(last - 1, g, (last - 1) % 2): (last, g, last % 2) for g in range(bands)}
    latent = lax.ppermute(latent, BOTH, full_pairs(edges, segments, bands, group, detour(last, bands)))
    parts = call(
        functools.partial(last_kernel, last, group, lon_local, turns),
        [part_shape] * bands,
        [latent, weights, gain, final_gain, decoder],
    )
    first = last % 2 ^ 1
    segment_id = lax.axis_index("segment")
    late, picked = set(), None
    ways = {k: fan_pairs(k, segments, bands, group, late) for k in range(bands - 1, -1, -1)}
    for k in (bands - 1, *range(bands - 1)):
        taken = lax.ppermute(parts[k], BOTH, ways[k])
        picked = taken if picked is None else jnp.where(place ^ segment_id ^ 1 == k, taken, picked)
    rows = [picked[c * lon_local : (c + 1) * lon_local] for c in range(group)]
    answer = rows[first]
    for e in range(1, group):
        handed = lax.ppermute(rows[first ^ e], BOTH, everywhere(segments, lons, e))
        answer = jnp.where(member == first ^ e, handed, answer)
    return answer.astype(jnp.float32)[None, None]


def solution(mesh):
    in_specs = (
        P(None, None, "lon", None),
        P(),
        P("segment", None, None, None),
        P("segment", None),
        P(),
        P(),
    )
    out_specs = P("segment", None, "lon", None)
    return jax.shard_map(body, mesh=mesh, in_specs=in_specs, out_specs=out_specs, check_vma=False)
```

```python
import functools

import jax
import jax.numpy as jnp
from jax import lax
from jax.experimental import pallas as pl
from jax.experimental.pallas import tpu as pltpu
from jax.sharding import PartitionSpec as P

HEADS = 16
SOFTCAP = 5.0
EPSILON = 1e-06
BOTH = ("segment", "lon")
LOG2_E = 1.4426950408889634
FULL_ROWS = 128
EXCHANGE_FLOPS = 8 * 10**9
EARLY = 2
HBM_SPEC = pl.BlockSpec(memory_space=pltpu.HBM)
VMEM_SPEC = pl.BlockSpec(memory_space=pltpu.VMEM)


def matmul(left, right):
    rows = left.shape[0]
    times = max(1, FULL_ROWS // rows)
    if times > 1:
        left = jnp.concatenate([left] * times, axis=0)
    return jnp.dot(left, right, preferred_element_type=jnp.float32)[:rows]


def norm_rows(latent, gain):
    square = jnp.mean(latent * latent, axis=-1, keepdims=True)
    return (latent * lax.rsqrt(square + EPSILON) * gain).astype(jnp.bfloat16)


def attend(queries, keys, values):
    rows, width = queries.shape
    head_size = width // HEADS
    heads = min(4, HEADS)
    lanes = heads * head_size
    cuts = [slice(start, start + lanes) for start in range(0, width, lanes)]
    turned = keys.T
    key_head = lax.broadcasted_iota(jnp.int32, (lanes, rows), 0) // head_size
    value_head = lax.broadcasted_iota(jnp.int32, (rows, lanes), 1) // head_size
    row_head = lax.broadcasted_iota(jnp.int32, (heads * rows, lanes), 0) // rows
    lane_head = lax.broadcasted_iota(jnp.int32, (heads * rows, lanes), 1) // head_size
    same_head = jnp.where(row_head == lane_head, 1.0, 0.0).astype(jnp.bfloat16)
    scores = []
    for cut in cuts:
        part = turned[cut]
        block = [jnp.where(key_head == head, part, jnp.zeros_like(part)) for head in range(heads)]
        scores.append(
            jnp.dot(queries[:, cut], jnp.concatenate(block, axis=1), preferred_element_type=jnp.float32)
        )
    capped = jnp.tanh(jnp.concatenate(scores, axis=0) * (head_size ** (-0.5) / SOFTCAP))
    raised = jnp.exp2(capped * (SOFTCAP * LOG2_E)).astype(jnp.bfloat16)
    total = jnp.dot(raised, same_head, preferred_element_type=jnp.float32)
    outs = []
    for index, cut in enumerate(cuts):
        part = values[:, cut]
        block = [jnp.where(value_head == head, part, jnp.zeros_like(part)) for head in range(heads)]
        mine = slice(index * rows, (index + 1) * rows)
        mixed = jnp.dot(raised[mine], jnp.concatenate(block, axis=0), preferred_element_type=jnp.float32)
        outs.append((mixed / total[mine]).astype(jnp.bfloat16))
    return jnp.concatenate(outs, axis=-1)


def layer(latent, weights, gain):
    wide = latent.astype(jnp.float32)
    normed = norm_rows(wide, gain)
    queries, keys, values = [matmul(normed, weights(i)).astype(jnp.bfloat16) for i in range(3)]
    attended = attend(queries, keys, values)
    return (wide + matmul(attended, weights(3))).astype(jnp.bfloat16)


def leads(group, segment):
    return (lax.axis_index("segment") == segment) & (lax.rem(lax.axis_index("lon"), group) == segment % 2)


def load_kernel(segments, group, hint, weights, decoder, gain, final_gain, *rest):
    weights_out, decoder_out, gain_out, final_out, sems = rest
    segment = lax.axis_index("segment")
    leader = lax.rem(lax.axis_index("lon"), group) == lax.rem(segment, 2)

    def move(pairs):
        copies = [
            pltpu.make_async_copy(source, target, sems.at[index])
            for index, (source, target) in enumerate(pairs)
        ]
        for copy in copies:
            copy.start()
        for copy in copies:
            copy.wait()

    @pl.when(leader & (segment > 0))
    def _():
        move([(weights.at[i], weights_out.at[i]) for i in range(4)] + [(gain, gain_out)])

    @pl.when(leader & (segment == segments - 1))
    def _():
        move([(decoder, decoder_out), (final_gain, final_out)])


def load(segments, group, hint, arrays):
    return pl.pallas_call(
        functools.partial(load_kernel, segments, group),
        out_shape=[pltpu.VMEM(value.shape, value.dtype) for value in arrays],
        in_specs=[pl.BlockSpec(memory_space=pl.ANY)] + [HBM_SPEC] * len(arrays),
        out_specs=[VMEM_SPEC] * len(arrays),
        scratch_shapes=[pltpu.SemaphoreType.DMA((6,))],
        compiler_params=pltpu.CompilerParams(vmem_limit_bytes=1024 * 1024),
        cost_estimate=pl.CostEstimate(flops=0, bytes_accessed=16 * 1024 * 1024, transcendentals=0),
    )(hint, *[in_hbm(value) for value in arrays])


def piece_kernel(group, table, *refs):
    picked, other, outs = refs[: len(table)], refs[len(table)], refs[len(table) + 1 :]
    place, member = lax.axis_index("lon") // group, lax.rem(lax.axis_index("lon"), group)
    for row, mine, out in zip(table, picked, outs):
        out[...] = jnp.concatenate([mine[...], other[place ^ sent_way(row, member) ^ 1]], axis=0)


def sent_way(row, member):
    way = row[1]
    for c in range(1, len(row)):
        way = jnp.where(member == c, row[c ^ 1], way)
    return way


def exchange_table(groups, group):
    ways = [2, 1, *range(3, groups)]
    ways += [0] * (-len(ways) % group)
    return [ways[start : start + group] for start in range(0, len(ways), group)]


def first_kernel(group, *refs):
    pieces, (encoder, weights, gain, out) = refs[:-4], refs[-4:]

    @pl.when(leads(group, 0))
    def _():
        patches = jnp.concatenate([piece[...] for piece in pieces], axis=0)
        latent = jnp.dot(patches, encoder[...], preferred_element_type=jnp.float32).astype(jnp.bfloat16)
        out[...] = layer(latent, lambda i: weights[i], gain[...])


def middle_kernel(tick, group, latent, weights, gain, out):
    @pl.when(leads(group, tick))
    def _():
        out[...] = layer(latent[...], lambda i: weights[i], gain[...])


def last_kernel(tick, group, rows, turns, latent, weights, gain, final_gain, decoder, *outs):
    @pl.when(leads(group, tick))
    def _():
        mixed = layer(latent[...], lambda i: weights[i], gain[...])
        final = norm_rows(mixed.astype(jnp.float32), final_gain[...])
        decoded = jnp.dot(final, decoder[...], preferred_element_type=jnp.float32)
        for block, out in enumerate(outs):
            turn = turns[block] ^ 1 if block else 0
            starts = [(block * group + (c ^ turn)) * rows for c in range(group)]
            out[...] = jnp.concatenate([decoded[start : start + rows] for start in starts], axis=0).astype(out.dtype)


def in_hbm(value):
    return pltpu.with_memory_space_constraint(value, pltpu.HBM)


def in_vmem(value):
    return pltpu.with_memory_space_constraint(value, pltpu.VMEM)


def call(kernel, out_shape, operands, in_specs=None, scratch=()):
    return pl.pallas_call(
        kernel,
        out_shape=out_shape,
        in_specs=in_specs or [VMEM_SPEC] * len(operands),
        out_specs=jax.tree.map(lambda _: VMEM_SPEC, out_shape),
        scratch_shapes=list(scratch),
        compiler_params=pltpu.CompilerParams(vmem_limit_bytes=16 * 1024 * 1024),
    )(*operands)


def assign(cost):
    size = len(cost)
    row_price, column_price, owner = [0.0] * (size + 1), [0.0] * (size + 1), [0] * (size + 1)
    for row in range(1, size + 1):
        owner[0], column = row, 0
        slack, back, seen = [float("inf")] * (size + 1), [0] * (size + 1), [False] * (size + 1)
        while owner[column]:
            seen[column], at, low, best = True, owner[column], float("inf"), 0
            for other in range(1, size + 1):
                if not seen[other]:
                    left = cost[at - 1][other - 1] - row_price[at] - column_price[other]
                    if left < slack[other]:
                        slack[other], back[other] = left, column
                    if slack[other] < low:
                        low, best = slack[other], other
            for other in range(size + 1):
                if seen[other]:
                    row_price[owner[other]] += low
                    column_price[other] -= low
                else:
                    slack[other] -= low
            column = best
        while column:
            owner[column] = owner[back[column]]
            column = back[column]
    chosen = [0] * size
    for column in range(1, size + 1):
        chosen[owner[column] - 1] = column - 1
    return chosen


def apart(one, two):
    return bin(one[0] ^ two[0]).count("1") + abs(one[1] - two[1])


def full_pairs(edges, segments, groups, group, extra={}):
    devices = [(s, g, c) for s in range(segments) for g in range(groups) for c in range(group)]
    edges = extra | edges
    targets = set(edges.values())
    givers = [one for one in devices if one in targets and one not in edges]
    takers = [one for one in devices if one in edges and one not in targets]
    chosen = assign([[apart(one, two) + 0.0 for two in takers] for one in givers])
    links = edges | {one: takers[column] for one, column in zip(givers, chosen)}
    idle = [one for one in devices if one not in links]
    for s, g, c in idle:
        if (s, g, c ^ 1) in idle:
            links[(s, g, c)] = (s, g, c ^ 1)
    rest = [one for one in idle if one not in links]
    while rest:
        ring = rest[:2] if len(rest) != 3 else rest
        rest = rest[len(ring) :]
        for one, two in zip(ring, ring[1:] + ring[:1]):
            links[one] = two
    number = {one: index for index, one in enumerate(devices)}
    return [(number[one], number[two]) for one, two in links.items()]


def detour(tick, groups):
    links = {}
    here, there = tick % 2, (tick - 1) % 2
    for g in range(groups):
        links |= {(tick, g, here): (tick, g, here ^ 1), (tick, g, here ^ 1): (tick - 1, g, there ^ 1)}
        links |= {(tick - 1, g, there ^ 1): (tick - 1, g, there)}
    return links


def ring_up(devices, links, free):
    alone = []
    for one in devices:
        mate = (one[0], one[1], one[2] ^ 1)
        if mate in devices:
            links[one] = mate
        else:
            alone.append(one)
    while len(alone) > 1:
        one, two = min(
            ((one, two) for index, one in enumerate(alone) for two in alone[index + 1 :]), key=lambda pair: apart(*pair)
        )
        links[one], links[two] = two, one
        alone = [three for three in alone if three not in (one, two)]
    for one in alone:
        two = min((two for two in devices if two != one and two[2] == free), key=lambda two: apart(one, two))
        after = links[two]
        links[one], links[two], links[after] = two, after, one


def fan_pairs(k, segments, groups, group, late):
    last = segments - 1
    work = last % 2
    free = work ^ 1
    devices = [(s, g, c) for s in range(segments) for g in range(groups) for c in range(group)]
    links = {(last, g, work): (g ^ 1, g ^ k, free) for g in range(groups)}
    taken = list(links.values())
    for s, g, _ in taken:
        links[(s, g, free)] = (s, g, work)
    inside = [g for s, g, _ in taken if s == last]
    givers = [(s, g, work) for s, g, _ in taken if s != last]
    takers = [(last, g, work) for g in range(groups) if g not in inside]
    for one, column in zip(givers, assign([[apart(one, two) + 0.0 for two in takers] for one in givers])):
        links[one] = takers[column]
    idle = [one for one in devices if one not in links]
    ring_up([one for one in idle if one not in late], links, free)
    ring_up([one for one in idle if one in late], links, free)
    late |= {(s, g, c) for s, g, _ in taken for c in range(2)} - {(last, g, work) for g in range(groups)}
    number = {one: index for index, one in enumerate(devices)}
    assert len(set(links.values())) == len(links) == len(devices)
    return [(number[one], number[two]) for one, two in links.items()]


def everywhere(segments, lons, mask):
    return [(s * lons + i, s * lons + (i ^ mask)) for s in range(segments) for i in range(lons)]


def body(patches, encoder_weight, layer_weights, layer_gains, final_gain, decoder_weight):
    segments = lax.axis_size("segment")
    lons = lax.axis_size("lon")
    bands, band_rows, lon_local, patch_values = patches.shape
    assert band_rows == 1 and bands == segments and lons % bands == 0
    assert lons & (lons - 1) == 0 and bands & (bands - 1) == 0 and 2 < bands < lons
    group = lons // bands
    columns = lons * lon_local
    width = encoder_weight.shape[1]
    out_values = decoder_weight.shape[1]

    place, member = lax.axis_index("lon") // group, lax.axis_index("lon") % group
    table = exchange_table(bands, group)
    rows_sent = [[0] * group] + table
    own = patches[:, 0]
    step = 1
    while step < group:
        other = lax.ppermute(own, BOTH, everywhere(segments, lons, step))
        picked = [
            lax.dynamic_index_in_dim(own, place ^ sent_way(row, member) ^ 1, 0, keepdims=False) for row in rows_sent
        ]
        picked = lax.optimization_barrier(picked) if step == 1 else picked
        own = jnp.concatenate([own, other], axis=1)
        step *= 2
    sent = pl.pallas_call(
        functools.partial(piece_kernel, group, rows_sent),
        out_shape=[jax.ShapeDtypeStruct((group * lon_local, patch_values), jnp.bfloat16)] * len(rows_sent),
        in_specs=[VMEM_SPEC] * (len(rows_sent) + 1),
        out_specs=[VMEM_SPEC] * len(rows_sent),
        compiler_params=pltpu.CompilerParams(vmem_limit_bytes=2 * 1024 * 1024),
        cost_estimate=pl.CostEstimate(flops=EXCHANGE_FLOPS, bytes_accessed=10**6, transcendentals=0),
    )(*picked, other)
    pieces = [sent[0]] + [None] * (bands - 1)
    turns = [1] + [0] * (bands - 1)
    for row, piece in zip(table, sent[1:]):
        pairs = [
            ((s * bands + g) * group + c, (s * bands + (g ^ row[c ^ 1])) * group + (c ^ 1))
            for s in range(segments)
            for g in range(bands)
            for c in range(group)
        ]
        taken = lax.ppermute(piece, BOTH, pairs)
        for c in range(group):
            if row[c]:
                pieces[row[c]] = lax.ppermute(taken, BOTH, everywhere(segments, lons, c)) if c else taken
                turns[row[c]] = c
    loaded = load(segments, group, pieces[0], [layer_weights[0], decoder_weight, layer_gains, final_gain[None]])
    weights, decoder, gain, final_gain = [in_vmem(value) for value in loaded]

    latent_shape = jax.ShapeDtypeStruct((columns, width), jnp.bfloat16)
    part_shape = jax.ShapeDtypeStruct((group * lon_local, out_values), jnp.bfloat16)
    first = [in_vmem(value) for value in (encoder_weight, layer_weights[0], layer_gains)]
    latent = call(functools.partial(first_kernel, group), latent_shape, pieces + first)
    for tick in range(1, segments - 1):
        edges = {(tick - 1, g, (tick - 1) % 2): (tick, g, tick % 2) for g in range(bands)}
        latent = lax.ppermute(latent, BOTH, full_pairs(edges, segments, bands, group, detour(tick, bands)))
        latent = call(functools.partial(middle_kernel, tick, group), latent_shape, [latent, weights, gain])
    last = segments - 1
    edges = {(last - 1, g, (last - 1) % 2): (last, g, last % 2) for g in range(bands)}
    latent = lax.ppermute(latent, BOTH, full_pairs(edges, segments, bands, group, detour(last, bands)))
    parts = call(
        functools.partial(last_kernel, last, group, lon_local, turns),
        [part_shape] * bands,
        [latent, weights, gain, final_gain, decoder],
    )
    first = last % 2 ^ 1
    segment_id = lax.axis_index("segment")
    late, picked = set(), None
    ways = {k: fan_pairs(k, segments, bands, group, late) for k in range(bands - 1, -1, -1)}
    for k in (bands - 1, *range(bands - 1)):
        taken = lax.ppermute(parts[k], BOTH, ways[k])
        picked = taken if picked is None else jnp.where(place ^ segment_id ^ 1 == k, taken, picked)
    rows = [picked[c * lon_local : (c + 1) * lon_local] for c in range(group)]
    answer = rows[first]
    for e in range(1, group):
        handed = lax.ppermute(rows[first ^ e], BOTH, everywhere(segments, lons, e))
        answer = jnp.where(member == first ^ e, handed, answer)
    return answer.astype(jnp.float32)[None, None]


def solution(mesh):
    in_specs = (
        P(None, None, "lon", None),
        P(),
        P("segment", None, None, None),
        P("segment", None),
        P(),
        P(),
    )
    out_specs = P("segment", None, "lon", None)
    return jax.shard_map(body, mesh=mesh, in_specs=in_specs, out_specs=out_specs, check_vma=False)
```

```python
import functools

import jax
import jax.numpy as jnp
from jax import lax
from jax.experimental import pallas as pl
from jax.experimental.pallas import tpu as pltpu
from jax.sharding import PartitionSpec as P

HEADS = 16
SOFTCAP = 5.0
EPSILON = 1e-06
BOTH = ("segment", "lon")
LOG2_E = 1.4426950408889634
FULL_ROWS = 128
EXCHANGE_FLOPS = 5 * 10**9
EARLY = 2
HBM_SPEC = pl.BlockSpec(memory_space=pltpu.HBM)
VMEM_SPEC = pl.BlockSpec(memory_space=pltpu.VMEM)


def matmul(left, right):
    rows = left.shape[0]
    times = max(1, FULL_ROWS // rows)
    if times > 1:
        left = jnp.concatenate([left] * times, axis=0)
    return jnp.dot(left, right, preferred_element_type=jnp.float32)[:rows]


def norm_rows(latent, gain):
    square = jnp.mean(latent * latent, axis=-1, keepdims=True)
    return (latent * lax.rsqrt(square + EPSILON) * gain).astype(jnp.bfloat16)


def attend(queries, keys, values):
    rows, width = queries.shape
    head_size = width // HEADS
    heads = min(4, HEADS)
    lanes = heads * head_size
    cuts = [slice(start, start + lanes) for start in range(0, width, lanes)]
    turned = keys.T
    key_head = lax.broadcasted_iota(jnp.int32, (lanes, rows), 0) // head_size
    value_head = lax.broadcasted_iota(jnp.int32, (rows, lanes), 1) // head_size
    row_head = lax.broadcasted_iota(jnp.int32, (heads * rows, lanes), 0) // rows
    lane_head = lax.broadcasted_iota(jnp.int32, (heads * rows, lanes), 1) // head_size
    same_head = jnp.where(row_head == lane_head, 1.0, 0.0).astype(jnp.bfloat16)
    scores = []
    for cut in cuts:
        part = turned[cut]
        block = [jnp.where(key_head == head, part, jnp.zeros_like(part)) for head in range(heads)]
        scores.append(
            jnp.dot(queries[:, cut], jnp.concatenate(block, axis=1), preferred_element_type=jnp.float32)
        )
    capped = jnp.tanh(jnp.concatenate(scores, axis=0) * (head_size ** (-0.5) / SOFTCAP))
    raised = jnp.exp2(capped * (SOFTCAP * LOG2_E)).astype(jnp.bfloat16)
    total = jnp.dot(raised, same_head, preferred_element_type=jnp.float32)
    outs = []
    for index, cut in enumerate(cuts):
        part = values[:, cut]
        block = [jnp.where(value_head == head, part, jnp.zeros_like(part)) for head in range(heads)]
        mine = slice(index * rows, (index + 1) * rows)
        mixed = jnp.dot(raised[mine], jnp.concatenate(block, axis=0), preferred_element_type=jnp.float32)
        outs.append((mixed / total[mine]).astype(jnp.bfloat16))
    return jnp.concatenate(outs, axis=-1)


def layer(latent, weights, gain):
    wide = latent.astype(jnp.float32)
    normed = norm_rows(wide, gain)
    keys, queries, values = [matmul(normed, weights(i)).astype(jnp.bfloat16) for i in (1, 0, 2)]
    attended = attend(queries, keys, values)
    return (wide + matmul(attended, weights(3))).astype(jnp.bfloat16)


def leads(group, segment):
    return (lax.axis_index("segment") == segment) & (lax.rem(lax.axis_index("lon"), group) == segment % 2)


def load_kernel(segments, group, hint, weights, decoder, gain, final_gain, *rest):
    weights_out, decoder_out, gain_out, final_out, sems = rest
    segment = lax.axis_index("segment")
    leader = lax.rem(lax.axis_index("lon"), group) == lax.rem(segment, 2)

    def move(pairs):
        copies = [
            pltpu.make_async_copy(source, target, sems.at[index])
            for index, (source, target) in enumerate(pairs)
        ]
        for copy in copies:
            copy.start()
        for copy in copies:
            copy.wait()

    @pl.when(leader & (segment > 0))
    def _():
        move([(weights.at[i], weights_out.at[i]) for i in range(4)] + [(gain, gain_out)])

    @pl.when(leader & (segment == segments - 1))
    def _():
        move([(decoder, decoder_out), (final_gain, final_out)])


def load(segments, group, hint, arrays):
    return pl.pallas_call(
        functools.partial(load_kernel, segments, group),
        out_shape=[pltpu.VMEM(value.shape, value.dtype) for value in arrays],
        in_specs=[pl.BlockSpec(memory_space=pl.ANY)] + [HBM_SPEC] * len(arrays),
        out_specs=[VMEM_SPEC] * len(arrays),
        scratch_shapes=[pltpu.SemaphoreType.DMA((6,))],
        compiler_params=pltpu.CompilerParams(vmem_limit_bytes=1024 * 1024),
        cost_estimate=pl.CostEstimate(flops=0, bytes_accessed=16 * 1024 * 1024, transcendentals=0),
    )(hint, *[in_hbm(value) for value in arrays])


def piece_kernel(group, table, *refs):
    picked, other, outs = refs[: len(table)], refs[len(table)], refs[len(table) + 1 :]
    place, member = lax.axis_index("lon") // group, lax.rem(lax.axis_index("lon"), group)
    for row, mine, out in zip(table, picked, outs):
        out[...] = jnp.concatenate([mine[...], other[place ^ sent_way(row, member) ^ 1]], axis=0)


def sent_way(row, member):
    way = row[1]
    for c in range(1, len(row)):
        way = jnp.where(member == c, row[c ^ 1], way)
    return way


def exchange_table(groups, group):
    ways = [2, 1, *range(3, groups)]
    ways += [0] * (-len(ways) % group)
    return [ways[start : start + group] for start in range(0, len(ways), group)]


def first_kernel(group, *refs):
    pieces, (encoder, weights, gain, out) = refs[:-4], refs[-4:]

    @pl.when(leads(group, 0))
    def _():
        patches = jnp.concatenate([piece[...] for piece in pieces], axis=0)
        latent = matmul(patches, encoder[...]).astype(jnp.bfloat16)
        out[...] = layer(latent, lambda i: weights[i], gain[...])


def middle_kernel(tick, group, latent, weights, gain, out):
    @pl.when(leads(group, tick))
    def _():
        out[...] = layer(latent[...], lambda i: weights[i], gain[...])


def last_kernel(tick, group, rows, turns, latent, weights, gain, final_gain, decoder, *outs):
    @pl.when(leads(group, tick))
    def _():
        mixed = layer(latent[...], lambda i: weights[i], gain[...])
        final = norm_rows(mixed.astype(jnp.float32), final_gain[...])
        decoded = matmul(final, decoder[...])
        for block, out in enumerate(outs):
            turn = turns[block] ^ 1 if block else 0
            starts = [(block * group + (c ^ turn)) * rows for c in range(group)]
            out[...] = jnp.concatenate([decoded[start : start + rows] for start in starts], axis=0).astype(out.dtype)


def in_hbm(value):
    return pltpu.with_memory_space_constraint(value, pltpu.HBM)


def in_vmem(value):
    return pltpu.with_memory_space_constraint(value, pltpu.VMEM)


def call(kernel, out_shape, operands, in_specs=None, scratch=()):
    return pl.pallas_call(
        kernel,
        out_shape=out_shape,
        in_specs=in_specs or [VMEM_SPEC] * len(operands),
        out_specs=jax.tree.map(lambda _: VMEM_SPEC, out_shape),
        scratch_shapes=list(scratch),
        compiler_params=pltpu.CompilerParams(vmem_limit_bytes=16 * 1024 * 1024),
    )(*operands)


def assign(cost):
    size = len(cost)
    row_price, column_price, owner = [0.0] * (size + 1), [0.0] * (size + 1), [0] * (size + 1)
    for row in range(1, size + 1):
        owner[0], column = row, 0
        slack, back, seen = [float("inf")] * (size + 1), [0] * (size + 1), [False] * (size + 1)
        while owner[column]:
            seen[column], at, low, best = True, owner[column], float("inf"), 0
            for other in range(1, size + 1):
                if not seen[other]:
                    left = cost[at - 1][other - 1] - row_price[at] - column_price[other]
                    if left < slack[other]:
                        slack[other], back[other] = left, column
                    if slack[other] < low:
                        low, best = slack[other], other
            for other in range(size + 1):
                if seen[other]:
                    row_price[owner[other]] += low
                    column_price[other] -= low
                else:
                    slack[other] -= low
            column = best
        while column:
            owner[column] = owner[back[column]]
            column = back[column]
    chosen = [0] * size
    for column in range(1, size + 1):
        chosen[owner[column] - 1] = column - 1
    return chosen


def apart(one, two):
    return bin(one[0] ^ two[0]).count("1") + abs(one[1] - two[1])


def full_pairs(edges, segments, groups, group, extra={}):
    devices = [(s, g, c) for s in range(segments) for g in range(groups) for c in range(group)]
    edges = extra | edges
    targets = set(edges.values())
    givers = [one for one in devices if one in targets and one not in edges]
    takers = [one for one in devices if one in edges and one not in targets]
    chosen = assign([[apart(one, two) + 0.0 for two in takers] for one in givers])
    links = edges | {one: takers[column] for one, column in zip(givers, chosen)}
    idle = [one for one in devices if one not in links]
    for s, g, c in idle:
        if (s, g, c ^ 1) in idle:
            links[(s, g, c)] = (s, g, c ^ 1)
    rest = [one for one in idle if one not in links]
    while rest:
        ring = rest[:2] if len(rest) != 3 else rest
        rest = rest[len(ring) :]
        for one, two in zip(ring, ring[1:] + ring[:1]):
            links[one] = two
    number = {one: index for index, one in enumerate(devices)}
    return [(number[one], number[two]) for one, two in links.items()]


def detour(tick, groups):
    links = {}
    here, there = tick % 2, (tick - 1) % 2
    for g in range(groups):
        links |= {(tick, g, here): (tick, g, here ^ 1), (tick, g, here ^ 1): (tick - 1, g, there ^ 1)}
        links |= {(tick - 1, g, there ^ 1): (tick - 1, g, there)}
    return links


def ring_up(devices, links, free):
    alone = []
    for one in devices:
        mate = (one[0], one[1], one[2] ^ 1)
        if mate in devices:
            links[one] = mate
        else:
            alone.append(one)
    while len(alone) > 1:
        one, two = min(
            ((one, two) for index, one in enumerate(alone) for two in alone[index + 1 :]), key=lambda pair: apart(*pair)
        )
        links[one], links[two] = two, one
        alone = [three for three in alone if three not in (one, two)]
    for one in alone:
        two = min((two for two in devices if two != one and two[2] == free), key=lambda two: apart(one, two))
        after = links[two]
        links[one], links[two], links[after] = two, after, one


def fan_pairs(k, segments, groups, group, late):
    last = segments - 1
    work = last % 2
    free = work ^ 1
    devices = [(s, g, c) for s in range(segments) for g in range(groups) for c in range(group)]
    links = {(last, g, work): (g ^ 1, g ^ k, free) for g in range(groups)}
    taken = list(links.values())
    for s, g, _ in taken:
        links[(s, g, free)] = (s, g, work)
    inside = [g for s, g, _ in taken if s == last]
    givers = [(s, g, work) for s, g, _ in taken if s != last]
    takers = [(last, g, work) for g in range(groups) if g not in inside]
    waiting = [one for one in sorted(late) if one[0] == last and one not in links]
    if len(waiting) % 2 and len(waiting) < groups - 1:
        one = waiting[0]
        links[one] = (last, one[1], work)
        takers[takers.index(links[one])] = one
    for one, column in zip(givers, assign([[apart(one, two) + 0.0 for two in takers] for one in givers])):
        links[one] = takers[column]
    idle = [one for one in devices if one not in links]
    ring_up([one for one in idle if one not in late], links, free)
    ring_up([one for one in idle if one in late], links, free)
    late |= {(s, g, c) for s, g, _ in taken for c in range(2)} - {(last, g, work) for g in range(groups)}
    number = {one: index for index, one in enumerate(devices)}
    assert len(set(links.values())) == len(links) == len(devices)
    return [(number[one], number[two]) for one, two in links.items()]


def everywhere(segments, lons, mask):
    return [(s * lons + i, s * lons + (i ^ mask)) for s in range(segments) for i in range(lons)]


def body(patches, encoder_weight, layer_weights, layer_gains, final_gain, decoder_weight):
    segments = lax.axis_size("segment")
    lons = lax.axis_size("lon")
    bands, band_rows, lon_local, patch_values = patches.shape
    assert band_rows == 1 and bands == segments and lons % bands == 0
    assert lons & (lons - 1) == 0 and bands & (bands - 1) == 0 and 2 < bands < lons
    group = lons // bands
    columns = lons * lon_local
    width = encoder_weight.shape[1]
    out_values = decoder_weight.shape[1]

    place, member = lax.axis_index("lon") // group, lax.axis_index("lon") % group
    table = exchange_table(bands, group)
    rows_sent = [[0] * group] + table
    own = patches[:, 0]
    step = 1
    while step < group:
        other = lax.ppermute(own, BOTH, everywhere(segments, lons, step))
        picked = [
            lax.dynamic_index_in_dim(own, place ^ sent_way(row, member) ^ 1, 0, keepdims=False) for row in rows_sent
        ]
        picked = lax.optimization_barrier(picked) if step == 1 else picked
        own = jnp.concatenate([own, other], axis=1)
        step *= 2
    sent = pl.pallas_call(
        functools.partial(piece_kernel, group, rows_sent),
        out_shape=[jax.ShapeDtypeStruct((group * lon_local, patch_values), jnp.bfloat16)] * len(rows_sent),
        in_specs=[VMEM_SPEC] * (len(rows_sent) + 1),
        out_specs=[VMEM_SPEC] * len(rows_sent),
        compiler_params=pltpu.CompilerParams(vmem_limit_bytes=2 * 1024 * 1024),
        cost_estimate=pl.CostEstimate(flops=EXCHANGE_FLOPS, bytes_accessed=10**6, transcendentals=0),
    )(*picked, other)
    pieces = [sent[0]] + [None] * (bands - 1)
    turns = [1] + [0] * (bands - 1)
    for row, piece in zip(table, sent[1:]):
        pairs = [
            ((s * bands + g) * group + c, (s * bands + (g ^ row[c ^ 1])) * group + (c ^ 1))
            for s in range(segments)
            for g in range(bands)
            for c in range(group)
        ]
        taken = lax.ppermute(piece, BOTH, pairs)
        for c in range(group):
            if row[c]:
                pieces[row[c]] = lax.ppermute(taken, BOTH, everywhere(segments, lons, c)) if c else taken
                turns[row[c]] = c
    loaded = load(segments, group, pieces[0], [layer_weights[0], decoder_weight, layer_gains, final_gain[None]])
    weights, decoder, gain, final_gain = [in_vmem(value) for value in loaded]

    latent_shape = jax.ShapeDtypeStruct((columns, width), jnp.bfloat16)
    part_shape = jax.ShapeDtypeStruct((group * lon_local, out_values), jnp.bfloat16)
    first = [in_vmem(value) for value in (encoder_weight, layer_weights[0], layer_gains)]
    latent = call(functools.partial(first_kernel, group), latent_shape, pieces + first)
    for tick in range(1, segments - 1):
        edges = {(tick - 1, g, (tick - 1) % 2): (tick, g, tick % 2) for g in range(bands)}
        latent = lax.ppermute(latent, BOTH, full_pairs(edges, segments, bands, group, detour(tick, bands)))
        latent = call(functools.partial(middle_kernel, tick, group), latent_shape, [latent, weights, gain])
    last = segments - 1
    edges = {(last - 1, g, (last - 1) % 2): (last, g, last % 2) for g in range(bands)}
    latent = lax.ppermute(latent, BOTH, full_pairs(edges, segments, bands, group, detour(last, bands)))
    parts = call(
        functools.partial(last_kernel, last, group, lon_local, turns),
        [part_shape] * bands,
        [latent, weights, gain, final_gain, decoder],
    )
    first = last % 2 ^ 1
    segment_id = lax.axis_index("segment")
    late, picked = set(), None
    ways = {k: fan_pairs(k, segments, bands, group, late) for k in range(bands - 1, -1, -1)}
    for k in (bands - 1, *range(bands - 1)):
        taken = lax.ppermute(parts[k], BOTH, ways[k])
        picked = taken if picked is None else jnp.where(place ^ segment_id ^ 1 == k, taken, picked)
    rows = [picked[c * lon_local : (c + 1) * lon_local] for c in range(group)]
    answer = rows[first]
    for e in range(1, group):
        handed = lax.ppermute(rows[first ^ e], BOTH, everywhere(segments, lons, e))
        answer = jnp.where(member == first ^ e, handed, answer)
    return answer.astype(jnp.float32)[None, None]


def solution(mesh):
    in_specs = (
        P(None, None, "lon", None),
        P(),
        P("segment", None, None, None),
        P("segment", None),
        P(),
        P(),
    )
    out_specs = P("segment", None, "lon", None)
    return jax.shard_map(body, mesh=mesh, in_specs=in_specs, out_specs=out_specs, check_vma=False)
```
